512 devices in a mesh: tm: 32 (over x, y, core), group: 16 (over z).
Axes of the slice: x: 4, y: 4, z: 16, core: 2. Of those that a mesh axis runs over, the one named last changes fastest.
Arguments:
- propagators: float32 [32, 384, 384], P('tm'), may hold values from -1 to 1, as said below
- perturbation: float32 [32, 384, 384], P('tm', 'group'), as said below
Outputs:
- gradient: float32 [384, 384], P('tm')
The draws below stay inside these ranges and needn't reach their ends.
Inputs may be any that keep to these rules, and one draw needn't show every extreme that they name: `propagators`: each slice's matrix is orthogonal. `perturbation`: each slice's matrix is symmetric.
All inputs are finite; a program needn't handle non-finite values.
Results may differ from the reference program's by a relative error of at most 0.00028.
Values sent between devices are 32-bit elements; how exact they have to be, the bound alone decides.
A program may use at most 128 MiB of HBM per device.

```python
import math
import jax
import jax.numpy as jnp
from jax import lax

D = 384
SLICES = 32


def draw_propagators(key, part):
    keys = jax.random.split(jax.random.fold_in(key, 11), SLICES)

    def single(one_key):
        raw = jax.random.normal(one_key, (D, D), jnp.float32)
        return jnp.linalg.qr(raw)[0]
    return jax.vmap(single)(keys)


def draw_perturbation(key, part):
    base_key = jax.random.fold_in(key, 7)
    raw = jax.random.normal(base_key, (SLICES, D, D), jnp.float32)
    return (raw + jnp.swapaxes(raw, 1, 2)) * (0.5 / math.sqrt(SLICES))


def setup_inputs(seed: int = 0) -> dict:
    streams_of = jax.random.split(jax.random.key(seed), 3)
    propagators = draw_propagators(jax.random.fold_in(streams_of[2], 71), 0)
    perturbation = draw_perturbation(jax.random.fold_in(streams_of[2], 71), 0)
    return {"propagators": propagators, "perturbation": perturbation}


def times_high(left, right):
    return jnp.dot(left.astype(jnp.float32), right.astype(jnp.float32), precision=lax.Precision.HIGHEST, preferred_element_type=jnp.float32)

def reference(propagators, perturbation):
    order_dim = propagators.shape[1]

    def advance(carry, pieces):
        before, total = carry
        propagator, symmetric = pieces
        pulled = times_high(symmetric, before)
        total = total + times_high(before.T, pulled)
        return ((times_high(propagator, before), total), None)
    start_carry = (jnp.eye(order_dim, dtype=jnp.float32), jnp.zeros((order_dim, order_dim), jnp.float32))
    (ending, gradient), unused = lax.scan(advance, start_carry, (propagators, perturbation))
    return gradient
```

```python
import jax
import jax.numpy as jnp
from jax import lax
from jax.experimental import pallas as pl
from jax.experimental.pallas import tpu as pltpu
from jax.sharding import Mesh
from jax.sharding import PartitionSpec as P

AXES = ("x", "y", "c", "z")
MESH = pl.DeviceIdType.MESH
F32 = jnp.float32
BF16 = jnp.bfloat16
D = 384
HALF = D // 2
CHUNK = HALF // 2
NX = 4
NY = 4
NZ = 16
HB = D // NZ
ROWS = D // 32
PIECE = 16
WIDE = 8 * PIECE
NN = ((1,), (0,))
NT = ((1,), (1,))
TN = ((0,), (0,))


def parts(value):
    high = value.astype(BF16)
    return high, (value - high.astype(F32)).astype(BF16)


def bdot(left, right, dims):
    return lax.dot_general(left, right, (dims, ((), ())), preferred_element_type=F32)


def times(left, right, dims=NN):
    lh, ll = parts(left)
    rh, rl = parts(right)
    if dims is TN:
        return bdot(lh, rh, dims) + (bdot(ll, rh, dims) + bdot(lh, rl, dims))
    n = left.shape[0]
    both = bdot(jnp.concatenate([lh, ll], axis=0), rh, dims)
    return both[:n] + (both[n:] + bdot(lh, rl, dims))


def kernel(a_ref, h_ref, o_ref, ao, s_buf, r_buf, h_buf, l_buf, z_buf, u_buf, g_buf, e_buf,
           a_sem, ys_sem, yr_sem, yd_sem, ye_sem, xs_sem, xr_sem, xd_sem, xe_sem,
           hs_sem, hr_sem, gs_sem, gr_sem, es_sem, er_sem):
    x, y, c, z = (lax.axis_index(a) for a in AXES)
    xr, xl, xo = (lax.rem(x + k, NX) for k in (1, 3, 2))
    yr, yl, yo = (lax.rem(y + k, NY) for k in (1, 3, 2))
    zr, zl, zo = (lax.rem(z + k, NZ) for k in (1, NZ - 1, 2))
    sib = (x, y, 1 - c, z)
    right_y, left_y = (x, yr, c, z), (x, yl, c, z)
    right_x, left_x = (xr, y, c, z), (xl, y, c, z)
    right_z, left_z = (x, y, c, zr), (x, y, c, zl)

    barrier = pltpu.get_barrier_semaphore()
    for dev in (sib, right_y, left_y, right_x, left_x, right_z, left_z):
        pl.semaphore_signal(barrier, 1, device_id=dev, device_id_type=MESH)
    pl.semaphore_wait(barrier, 7)

    def remote(src, dst, send, recv, dev):
        return pltpu.make_async_remote_copy(
            src_ref=src, dst_ref=dst, send_sem=send, recv_sem=recv, device_id=dev, device_id_type=MESH)

    a_copy = remote(a_ref.at[0], ao, a_sem.at[0], a_sem.at[1], sib)
    a_copy.start()
    h_buf[pl.ds(z * HB, HB)] = h_ref[0]

    def h_block(k):
        return h_buf.at[pl.ds(lax.rem(z + k + NZ, NZ) * HB, HB)]

    def h_right(j):
        return remote(h_block(-j), h_block(-j), hs_sem.at[0, j], hr_sem.at[0, j], right_z)

    def h_left(j):
        return remote(h_block(j), h_block(j), hs_sem.at[1, j], hr_sem.at[1, j], left_z)

    def h_wait_right(j):
        remote(h_block(-j), h_block(-j), hs_sem.at[0, j - 1], hr_sem.at[0, j - 1], right_z).wait_recv()

    def h_wait_left(j):
        remote(h_block(j), h_block(j), hs_sem.at[1, j - 1], hr_sem.at[1, j - 1], left_z).wait_recv()

    def h_step(j):
        h_wait_right(j)
        if j < NZ // 2:
            h_right(j).start()
            h_wait_left(j)
            if j < NZ // 2 - 1:
                h_left(j).start()

    h_right(0).start()
    h_left(0).start()
    a_copy.wait_recv()

    half = pl.ds(c * HALF, HALF)

    @pl.when(c == 0)
    def _():
        s_buf[y, half] = times(ao[half], a_ref[0])

    @pl.when(c == 1)
    def _():
        s_buf[y, half] = times(a_ref[0, half], ao[...])

    def rows(k, core=None):
        return pl.ds((c if core is None else core) * HALF + k * CHUNK, CHUNK)

    def s_chunk(place, k):
        return s_buf.at[place, rows(k)]

    def y_copy(place, k, dev, n):
        return remote(s_chunk(place, k), s_chunk(place, k), ys_sem.at[n], yr_sem.at[n], dev)

    def y_share(place, k, n):
        return remote(s_chunk(place, k), s_chunk(place, k), yd_sem.at[n], ye_sem.at[n], sib)

    def y_shared(place, k, n):
        there = s_buf.at[place, rows(k, 1 - c)]
        return remote(there, there, yd_sem.at[n], ye_sem.at[n], sib)

    y_out = [
        y_copy(y, 0, right_y, 0), y_copy(y, 1, left_y, 3),
        y_copy(y, 1, right_y, 1), y_copy(y, 0, left_y, 2),
    ]
    for copy in y_out:
        copy.start()
    y_sh = []

    def share_s(place, k, n):
        copy = y_share(place, k, n)
        copy.start()
        y_sh.append((copy, y_shared(place, k, n)))

    share_s(y, 0, 6)
    share_s(y, 1, 7)
    h_step(1)
    y_copy(yl, 0, left_y, 0).wait_recv()
    copy = y_copy(yl, 0, right_y, 4)
    copy.start()
    y_out.append(copy)
    y_copy(yr, 1, right_y, 3).wait_recv()
    copy = y_copy(yr, 1, left_y, 5)
    copy.start()
    y_out.append(copy)
    share_s(yl, 0, 0)
    share_s(yr, 1, 3)
    h_step(2)
    y_copy(yl, 1, left_y, 1).wait_recv()
    share_s(yl, 1, 1)
    y_copy(yr, 0, left_y, 2).wait_recv()
    share_s(yr, 0, 2)
    h_step(3)
    y_copy(yo, 0, left_y, 4).wait_recv()
    share_s(yo, 0, 4)
    y_copy(yo, 1, left_y, 5).wait_recv()
    share_s(yo, 1, 5)
    for _, arrival in y_sh:
        arrival.wait_recv()

    @pl.when(x < NX - 1)
    def _():
        value = s_buf[3, half]
        for k in (2, 1, 0):
            value = times(value, s_buf[k])
        r_buf[x, half] = value

    def r_chunk(place, k):
        return r_buf.at[place, rows(k)]

    def x_copy(place, k, dev, n):
        return remote(r_chunk(place, k), r_chunk(place, k), xs_sem.at[n], xr_sem.at[n], dev)

    def x_share(place, k, n):
        return remote(r_chunk(place, k), r_chunk(place, k), xd_sem.at[n], xe_sem.at[n], sib)

    def x_shared(place, k, n):
        there = r_buf.at[place, rows(k, 1 - c)]
        return remote(there, there, xd_sem.at[n], xe_sem.at[n], sib)

    to_right = x < 3
    first = x == 0
    last = x == 3
    x_out = []

    def when_start(cond, copy):
        @pl.when(cond)
        def _():
            copy.start()
        x_out.append((cond, copy))

    def when_recv(cond, copy):
        @pl.when(cond)
        def _():
            copy.wait_recv()

    when_start(to_right, x_copy(x, 0, right_x, 0))
    when_start(x < 2, x_copy(x, 1, left_x, 3))
    when_start(to_right, x_copy(x, 1, right_x, 1))
    when_start(first, x_copy(x, 0, left_x, 2))
    h_step(4)

    @pl.when(y == 1)
    def _():
        l_buf[...] = s_buf[0]

    @pl.when(y >= 2)
    def _():
        l_buf[...] = times(s_buf[1], s_buf[0])

    x_sh = []

    def share_r(cond, place, k, n):
        copy = x_share(place, k, n)
        when_start(cond, copy)
        x_sh.append((cond, x_shared(place, k, n)))

    from_left = x > 0
    opposite = x > 1
    when_recv(from_left, x_copy(xl, 0, left_x, 0))
    when_start((x == 1) | (x == 2), x_copy(xl, 0, right_x, 4))
    when_recv(first | last, x_copy(xr, 1, right_x, 3))
    when_start(first | last, x_copy(xr, 1, left_x, 5))
    share_r(from_left, xl, 0, 0)
    share_r(last, xr, 1, 3)
    h_step(5)

    @pl.when(y == 3)
    def _():
        l_buf[...] = times(s_buf[2], l_buf[...])

    @pl.when((c == 1) & (y == 0))
    def _():
        l_buf[...] = ao[...]

    @pl.when((c == 1) & (y > 0))
    def _():
        l_buf[...] = times(ao[...], l_buf[...])

    h_step(6)
    when_recv(from_left, x_copy(xl, 1, left_x, 1))
    share_r(from_left, xl, 1, 1)
    when_recv(last, x_copy(xr, 0, left_x, 2))
    share_r(last, xr, 0, 2)
    h_step(7)
    when_recv(opposite, x_copy(xo, 0, left_x, 4))
    share_r(opposite, xo, 0, 4)
    when_recv(opposite, x_copy(xo, 1, left_x, 5))
    share_r(opposite, xo, 1, 5)
    h_step(8)

    inner = (y > 0) | (c > 0)

    @pl.when(jnp.logical_not(inner))
    def _():
        z_buf[...] = h_buf[...]

    @pl.when(inner)
    def _():
        z_buf[...] = times(l_buf[...], times(h_buf[...], l_buf[...]), TN)

    for cond, arrival in x_sh:
        when_recv(cond, arrival)

    part = lax.rem(z, 4)
    place = lax.broadcasted_iota(jnp.int32, (WIDE, D), 0)
    column = lax.broadcasted_iota(jnp.int32, (WIDE, D), 1)
    within = place & (PIECE - 1)
    wanted = part * (8 * ROWS) + (place >> 4) * ROWS + within
    u_buf[...] = jnp.where((within < ROWS) & (column == wanted), 1.0, 0.0).astype(F32)
    for k in range(NX - 1):
        @pl.when(x > k)
        def _(k=k):
            u_buf[...] = times(u_buf[...], r_buf[k], NT)
    u_buf[...] = times(u_buf[...], z_buf[...])
    for k in reversed(range(NX - 1)):
        @pl.when(x > k)
        def _(k=k):
            u_buf[...] = times(u_buf[...], r_buf[k])

    me = (x * NY + y) * 2 + c
    owner = x == part
    g_out = []
    for p in range(8):
        mine = owner & (y * 2 + c == p)
        copy = remote(u_buf.at[pl.ds(p * PIECE, PIECE)], g_buf.at[me], gs_sem.at[p], gr_sem.at[me],
                      (part, p // 2, p % 2, z))

        @pl.when(mine)
        def _(p=p):
            g_buf[me] = u_buf[pl.ds(p * PIECE, PIECE)]

        @pl.when(jnp.logical_not(mine))
        def _(copy=copy):
            copy.start()
        g_out.append((jnp.logical_not(mine), copy))

    e_out = [remote(e_buf.at[0], e_buf.at[1], es_sem.at[k], er_sem.at[0], (x, y, c, dev))
             for k, dev in enumerate((zr, zl, zo))]

    @pl.when(owner)
    def _():
        for s in range(32):
            @pl.when(s != me)
            def _(s=s):
                remote(g_buf.at[s], g_buf.at[s], gs_sem.at[0], gr_sem.at[s], sib).wait_recv()
        total = g_buf[0]
        for s in range(1, 32):
            total = total + g_buf[s]
        e_buf[0] = total
        for copy in e_out:
            copy.start()
        o_ref[...] = total[:ROWS]
        for copy in e_out:
            copy.wait_send()

    @pl.when(jnp.logical_not(owner))
    def _():
        e_out[0].wait_recv()
        o_ref[...] = e_buf[1, :ROWS]

    a_copy.wait_send()
    for j in range(NZ // 2):
        h_right(j).wait_send()
    for j in range(NZ // 2 - 1):
        h_left(j).wait_send()
    for copy in y_out:
        copy.wait_send()
    for copy, _ in y_sh:
        copy.wait_send()
    for cond, copy in x_out + g_out:
        @pl.when(cond)
        def _(copy=copy):
            copy.wait_send()


def body(propagators, perturbation):
    full = pltpu.VMEM((D, D), F32)
    dma = pltpu.SemaphoreType.DMA
    return pl.pallas_call(
        kernel,
        out_shape=jax.ShapeDtypeStruct((ROWS, D), F32),
        in_specs=[pl.BlockSpec(memory_space=pltpu.VMEM)] * 2,
        out_specs=pl.BlockSpec(memory_space=pltpu.VMEM),
        scratch_shapes=[
            full,
            pltpu.VMEM((NY, D, D), F32),
            pltpu.VMEM((NX, D, D), F32),
            full,
            full,
            full,
            pltpu.VMEM((WIDE, D), F32),
            pltpu.VMEM((32, PIECE, D), F32),
            pltpu.VMEM((2, PIECE, D), F32),
            dma((2,)),
            dma((6,)), dma((6,)), dma((8,)), dma((8,)),
            dma((6,)), dma((6,)), dma((6,)), dma((6,)),
            dma((2, 8)), dma((2, 8)),
            dma((8,)), dma((32,)),
            dma((3,)), dma((1,)),
        ],
        compiler_params=pltpu.CompilerParams(
            collective_id=0, has_side_effects=True, vmem_limit_bytes=48 * 2**20),
        name="floquet",
    )(propagators, perturbation)


def solution(mesh):
    split = Mesh(mesh.devices.reshape(NX, NY, 2, NZ), AXES)
    tm = ("x", "y", "c")
    return jax.shard_map(
        body,
        mesh=split,
        in_specs=(P(tm, None, None), P(tm, "z", None)),
        out_specs=P(tm, None),
        check_vma=False,
    )
```

```python
import jax
import jax.numpy as jnp
from jax import lax
from jax.experimental import pallas as pl
from jax.experimental.pallas import tpu as pltpu
from jax.sharding import Mesh
from jax.sharding import PartitionSpec as P

AXES = ("x", "y", "c", "z")
MESH = pl.DeviceIdType.MESH
F32 = jnp.float32
BF16 = jnp.bfloat16
D = 384
HALF = D // 2
CHUNK = HALF // 2
NX = 4
NY = 4
NZ = 16
HB = D // NZ
ROWS = D // 32
PIECE = 16
WIDE = 4 * PIECE
NN = ((1,), (0,))
NT = ((1,), (1,))
TN = ((0,), (0,))


def parts(value):
    high = value.astype(BF16)
    return high, (value - high.astype(F32)).astype(BF16)


def bdot(left, right, dims):
    return lax.dot_general(left, right, (dims, ((), ())), preferred_element_type=F32)


def times(left, right, dims=NN):
    lh, ll = parts(left)
    rh, rl = parts(right)
    if dims is TN:
        return bdot(lh, rh, dims) + (bdot(ll, rh, dims) + bdot(lh, rl, dims))
    n = left.shape[0]
    both = bdot(jnp.concatenate([lh, ll], axis=0), rh, dims)
    return both[:n] + (both[n:] + bdot(lh, rl, dims))


def kernel(a_hbm, h_hbm, o_ref, av, ao, s_buf, r_buf, h_buf, l_buf, z_buf, zo_buf, u_buf, t_buf, v_buf, g_buf,
           in_sem, a_sem, ys_sem, yr_sem, yd_sem, ye_sem, xs_sem, xr_sem, xd_sem, xe_sem,
           hs_sem, hr_sem, zz_sem, ts_sem, tr_sem, gs_sem, gr_sem):
    x, y, c, z = (lax.axis_index(a) for a in AXES)
    a_load = pltpu.make_async_copy(a_hbm.at[0], av, in_sem.at[0])
    h_load = pltpu.make_async_copy(h_hbm.at[0], h_buf.at[pl.ds(z * HB, HB)], in_sem.at[1])
    a_load.start()
    h_load.start()
    xr, xl, xo = (lax.rem(x + k, NX) for k in (1, 3, 2))
    yr, yl, yo = (lax.rem(y + k, NY) for k in (1, 3, 2))
    zr, zl, zo = (lax.rem(z + k, NZ) for k in (1, NZ - 1, 2))
    sib = (x, y, 1 - c, z)
    right_y, left_y = (x, yr, c, z), (x, yl, c, z)
    right_x, left_x = (xr, y, c, z), (xl, y, c, z)
    right_z, left_z = (x, y, c, zr), (x, y, c, zl)

    barrier = pltpu.get_barrier_semaphore()
    for dev in (sib, right_y, left_y, right_x, left_x, right_z, left_z):
        pl.semaphore_signal(barrier, 1, device_id=dev, device_id_type=MESH)
    pl.semaphore_wait(barrier, 7)

    def remote(src, dst, send, recv, dev):
        return pltpu.make_async_remote_copy(
            src_ref=src, dst_ref=dst, send_sem=send, recv_sem=recv, device_id=dev, device_id_type=MESH)

    low, high = pl.ds(0, HALF), pl.ds(HALF, HALF)
    a_low = remote(av.at[low], ao.at[low], a_sem.at[0], a_sem.at[1], sib)
    a_high = remote(av.at[high], ao.at[high], a_sem.at[2], a_sem.at[3], sib)
    a_load.wait()
    a_low.start()

    @pl.when(c == 0)
    def _():
        a_high.start()
    h_load.wait()

    def h_block(k):
        return h_buf.at[pl.ds(lax.rem(z + k + NZ, NZ) * HB, HB)]

    def h_right(j):
        return remote(h_block(-j), h_block(-j), hs_sem.at[0, j], hr_sem.at[0, j], right_z)

    def h_left(j):
        return remote(h_block(j), h_block(j), hs_sem.at[1, j], hr_sem.at[1, j], left_z)

    def h_wait_right(j):
        remote(h_block(-j), h_block(-j), hs_sem.at[0, j - 1], hr_sem.at[0, j - 1], right_z).wait_recv()

    def h_wait_left(j):
        remote(h_block(j), h_block(j), hs_sem.at[1, j - 1], hr_sem.at[1, j - 1], left_z).wait_recv()

    def h_step(j):
        h_wait_right(j)
        if j < NZ // 2:
            h_right(j).start()
            h_wait_left(j)
            if j < NZ // 2 - 1:
                h_left(j).start()

    h_right(0).start()
    h_left(0).start()
    a_low.wait_recv()

    half = pl.ds(c * HALF, HALF)

    @pl.when(c == 0)
    def _():
        s_buf[y, low] = times(ao[low], av[...])

    @pl.when(c == 1)
    def _():
        a_high.wait_recv()
        s_buf[y, high] = times(av[high], ao[...])

    def rows(k, core=None):
        return pl.ds((c if core is None else core) * HALF + k * CHUNK, CHUNK)

    def s_chunk(place, k):
        return s_buf.at[place, rows(k)]

    def y_copy(place, k, dev, n):
        return remote(s_chunk(place, k), s_chunk(place, k), ys_sem.at[n], yr_sem.at[n], dev)

    def y_share(place, k, n):
        return remote(s_chunk(place, k), s_chunk(place, k), yd_sem.at[n], ye_sem.at[n], sib)

    def y_shared(place, k, n):
        there = s_buf.at[place, rows(k, 1 - c)]
        return remote(there, there, yd_sem.at[n], ye_sem.at[n], sib)

    y_out = [
        y_copy(y, 0, right_y, 0), y_copy(y, 1, left_y, 3),
        y_copy(y, 1, right_y, 1), y_copy(y, 0, left_y, 2),
    ]
    for copy in y_out:
        copy.start()
    y_sh = []

    def share_s(place, k, n):
        copy = y_share(place, k, n)
        copy.start()
        y_sh.append((copy, y_shared(place, k, n)))

    share_s(y, 0, 6)
    share_s(y, 1, 7)
    h_step(1)
    h_step(2)
    y_copy(yl, 0, left_y, 0).wait_recv()
    copy = y_copy(yl, 0, right_y, 4)
    copy.start()
    y_out.append(copy)
    y_copy(yr, 1, right_y, 3).wait_recv()
    copy = y_copy(yr, 1, left_y, 5)
    copy.start()
    y_out.append(copy)
    share_s(yl, 0, 0)
    share_s(yr, 1, 3)
    h_step(3)
    y_copy(yl, 1, left_y, 1).wait_recv()
    share_s(yl, 1, 1)
    y_copy(yr, 0, left_y, 2).wait_recv()
    share_s(yr, 0, 2)
    h_step(4)
    y_copy(yo, 0, left_y, 4).wait_recv()
    share_s(yo, 0, 4)
    y_copy(yo, 1, left_y, 5).wait_recv()
    share_s(yo, 1, 5)
    for _, arrival in y_sh:
        arrival.wait_recv()

    @pl.when(x < NX - 1)
    def _():
        value = s_buf[3, half]
        for k in (2, 1, 0):
            value = times(value, s_buf[k])
        r_buf[x, half] = value

    def r_chunk(place, k):
        return r_buf.at[place, rows(k)]

    def x_copy(place, k, dev, n):
        return remote(r_chunk(place, k), r_chunk(place, k), xs_sem.at[n], xr_sem.at[n], dev)

    def x_share(place, k, n):
        return remote(r_chunk(place, k), r_chunk(place, k), xd_sem.at[n], xe_sem.at[n], sib)

    def x_shared(place, k, n):
        there = r_buf.at[place, rows(k, 1 - c)]
        return remote(there, there, xd_sem.at[n], xe_sem.at[n], sib)

    to_right = x < 3
    first = x == 0
    last = x == 3
    x_out = []

    def when_start(cond, copy):
        @pl.when(cond)
        def _():
            copy.start()
        x_out.append((cond, copy))

    def when_recv(cond, copy):
        @pl.when(cond)
        def _():
            copy.wait_recv()

    when_start(to_right, x_copy(x, 0, right_x, 0))
    when_start(x < 2, x_copy(x, 1, left_x, 3))
    when_start(to_right, x_copy(x, 1, right_x, 1))
    when_start(first, x_copy(x, 0, left_x, 2))
    h_step(5)

    @pl.when(y == 1)
    def _():
        l_buf[...] = s_buf[0]

    @pl.when(y >= 2)
    def _():
        l_buf[...] = times(s_buf[1], s_buf[0])

    h_step(6)

    x_sh = []

    def share_r(cond, place, k, n):
        copy = x_share(place, k, n)
        when_start(cond, copy)
        x_sh.append((cond, x_shared(place, k, n)))

    from_left = x > 0
    opposite = x > 1
    when_recv(from_left, x_copy(xl, 0, left_x, 0))
    when_start((x == 1) | (x == 2), x_copy(xl, 0, right_x, 4))
    when_recv(first | last, x_copy(xr, 1, right_x, 3))
    when_start(first | last, x_copy(xr, 1, left_x, 5))
    share_r(from_left, xl, 0, 0)
    share_r(last, xr, 1, 3)
    h_step(7)

    @pl.when(y == 3)
    def _():
        l_buf[...] = times(s_buf[2], l_buf[...])

    @pl.when((c == 1) & (y == 0))
    def _():
        l_buf[...] = ao[...]

    @pl.when((c == 1) & (y > 0))
    def _():
        l_buf[...] = times(ao[...], l_buf[...])

    h_step(8)
    when_recv(from_left, x_copy(xl, 1, left_x, 1))
    share_r(from_left, xl, 1, 1)
    when_recv(last, x_copy(xr, 0, left_x, 2))
    share_r(last, xr, 0, 2)

    inner = (y > 0) | (c > 0)

    @pl.when(jnp.logical_not(inner))
    def _():
        z_buf[...] = h_buf[...]

    @pl.when(inner)
    def _():
        z_buf[...] = times(l_buf[...], times(h_buf[...], l_buf[...]), TN)

    z_copy = remote(z_buf, zo_buf, zz_sem.at[0], zz_sem.at[1], sib)
    z_copy.start()
    when_recv(opposite, x_copy(xo, 0, left_x, 4))
    share_r(opposite, xo, 0, 4)
    when_recv(opposite, x_copy(xo, 1, left_x, 5))
    share_r(opposite, xo, 1, 5)
    for cond, arrival in x_sh:
        when_recv(cond, arrival)

    part = lax.rem(z, 4)
    place = lax.broadcasted_iota(jnp.int32, (WIDE, D), 0)
    column = lax.broadcasted_iota(jnp.int32, (WIDE, D), 1)
    within = place & (PIECE - 1)
    wanted = part * (8 * ROWS) + (c * 4 + (place >> 4)) * ROWS + within
    u_buf[...] = jnp.where((within < ROWS) & (column == wanted), 1.0, 0.0).astype(F32)
    for k in range(NX - 1):
        @pl.when(x > k)
        def _(k=k):
            u_buf[...] = times(u_buf[...], r_buf[k], NT)
    z_copy.wait_recv()
    u_buf[...] = times(u_buf[...], z_buf[...] + zo_buf[...])

    t_out = []
    for q in range(4):
        yt, ct = c * 2 + q // 2, q % 2
        mine = (y == yt) & (c == ct)
        copy = remote(u_buf.at[pl.ds(q * PIECE, PIECE)], t_buf.at[y], ts_sem.at[q], tr_sem.at[y],
                      (x, yt, ct, z))

        @pl.when(mine)
        def _(q=q):
            t_buf[y] = u_buf[pl.ds(q * PIECE, PIECE)]

        @pl.when(jnp.logical_not(mine))
        def _(copy=copy):
            copy.start()
        t_out.append((jnp.logical_not(mine), copy))
    holder = c == lax.div(y, 2)
    for k in range(NY):
        @pl.when(jnp.logical_not(holder & (y == k)))
        def _(k=k):
            remote(t_buf.at[k], t_buf.at[k], ts_sem.at[0], tr_sem.at[k], sib).wait_recv()
    v_buf[...] = (t_buf[0] + t_buf[1]) + (t_buf[2] + t_buf[3])
    for k in reversed(range(NX - 1)):
        @pl.when(x > k)
        def _(k=k):
            v_buf[...] = times(v_buf[...], r_buf[k])

    for k, there in enumerate((z, zr, zl, zo)):
        copy = remote(v_buf, g_buf.at[x], gs_sem.at[k], gr_sem.at[x], (part, y, c, there))
        if k == 0:
            cond = x != part

            @pl.when(x == part)
            def _():
                g_buf[x] = v_buf[...]

            @pl.when(cond)
            def _(copy=copy):
                copy.start()
            t_out.append((cond, copy))
        else:
            copy.start()
            t_out.append((c < 2, copy))
    for k in range(NX):
        @pl.when(jnp.logical_not((x == part) & (x == k)))
        def _(k=k):
            remote(g_buf.at[k], g_buf.at[k], gs_sem.at[0], gr_sem.at[k], sib).wait_recv()
    total = (g_buf[0] + g_buf[1]) + (g_buf[2] + g_buf[3])
    o_ref[...] = total[:ROWS]

    a_low.wait_send()

    @pl.when(c == 0)
    def _():
        a_high.wait_send()
    z_copy.wait_send()
    for j in range(NZ // 2):
        h_right(j).wait_send()
    for j in range(NZ // 2 - 1):
        h_left(j).wait_send()
    for copy in y_out:
        copy.wait_send()
    for copy, _ in y_sh:
        copy.wait_send()
    for cond, copy in x_out + t_out:
        @pl.when(cond)
        def _(copy=copy):
            copy.wait_send()


def body(propagators, perturbation):
    full = pltpu.VMEM((D, D), F32)
    dma = pltpu.SemaphoreType.DMA
    return pl.pallas_call(
        kernel,
        out_shape=jax.ShapeDtypeStruct((ROWS, D), F32),
        in_specs=[pl.BlockSpec(memory_space=pltpu.HBM)] * 2,
        out_specs=pl.BlockSpec(memory_space=pltpu.VMEM),
        scratch_shapes=[
            full, full,
            pltpu.VMEM((NY, D, D), F32),
            pltpu.VMEM((NX, D, D), F32),
            full, full, full, full,
            pltpu.VMEM((WIDE, D), F32),
            pltpu.VMEM((NY, PIECE, D), F32),
            pltpu.VMEM((PIECE, D), F32),
            pltpu.VMEM((NX, PIECE, D), F32),
            dma((2,)), dma((4,)),
            dma((6,)), dma((6,)), dma((8,)), dma((8,)),
            dma((6,)), dma((6,)), dma((6,)), dma((6,)),
            dma((2, 8)), dma((2, 8)), dma((2,)),
            dma((4,)), dma((4,)),
            dma((4,)), dma((4,)),
        ],
        compiler_params=pltpu.CompilerParams(
            collective_id=0, has_side_effects=True, vmem_limit_bytes=60 * 2**20),
        name="floquet",
    )(propagators, perturbation)


def solution(mesh):
    split = Mesh(mesh.devices.reshape(NX, NY, 2, NZ), AXES)
    tm = ("x", "y", "c")
    return jax.shard_map(
        body,
        mesh=split,
        in_specs=(P(tm, None, None), P(tm, "z", None)),
        out_specs=P(tm, None),
        check_vma=False,
    )
```

```python
import jax
import jax.numpy as jnp
from jax import lax
from jax.experimental import pallas as pl
from jax.experimental.pallas import tpu as pltpu
from jax.sharding import Mesh
from jax.sharding import PartitionSpec as P

AXES = ("x", "y", "c", "z")
MESH = pl.DeviceIdType.MESH
F32 = jnp.float32
BF16 = jnp.bfloat16
D = 384
HALF = D // 2
CHUNK = HALF // 2
PART = CHUNK // 2
NX = 4
NY = 4
NZ = 16
NW = 4
HB = D // NZ
ROWS = D // 32
PIECE = 16
WIDE = 4 * PIECE
NN = ((1,), (0,))
NT = ((1,), (1,))
TN = ((0,), (0,))


def parts(value):
    high = value.astype(BF16)
    return high, (value - high.astype(F32)).astype(BF16)


def bdot(left, right, dims):
    return lax.dot_general(left, right, (dims, ((), ())), preferred_element_type=F32)


def times(left, right, dims=NN):
    lh, ll = parts(left)
    rh, rl = parts(right)
    if dims is TN:
        return bdot(lh, rh, dims) + (bdot(ll, rh, dims) + bdot(lh, rl, dims))
    n = left.shape[0]
    both = bdot(jnp.concatenate([lh, ll], axis=0), rh, dims)
    return both[:n] + (both[n:] + bdot(lh, rl, dims))


def kernel(a_hbm, h_hbm, o_ref, av, ao, s_buf, r_buf, h_buf, l_buf, z_buf, zo_buf, u_buf, t_buf, v_buf, g_buf, n_buf,
           e_buf, in_sem, a_sem, ys_sem, yr_sem, yd_sem, ye_sem, xs_sem, xr_sem, xd_sem, xe_sem,
           hs_sem, hr_sem, zz_sem, ts_sem, tr_sem, gs_sem, gr_sem, es_sem, er_sem):
    x, y, c, z = (lax.axis_index(a) for a in AXES)
    worker = z < NW
    owner = z == x
    here = pl.ds(z * HB, HB)
    a_load = pltpu.make_async_copy(a_hbm.at[0], av, in_sem.at[0])
    h_load = pltpu.make_async_copy(h_hbm.at[0], h_buf.at[here], in_sem.at[1])
    pl.when(worker)(a_load.start)
    h_load.start()
    xr, xl, xo = (lax.rem(x + k, NX) for k in (1, 3, 2))
    yr, yl, yo = (lax.rem(y + k, NY) for k in (1, 3, 2))
    others = [(x, y, c, lax.rem(z + k, NZ)) for k in range(1, NZ)]
    sib = (x, y, 1 - c, z)
    right_y, left_y = (x, yr, c, z), (x, yl, c, z)
    right_x, left_x = (xr, y, c, z), (xl, y, c, z)

    barrier = pltpu.get_barrier_semaphore()

    @pl.when(worker)
    def _():
        for dev in [sib, right_y, left_y, right_x, left_x] + others:
            pl.semaphore_signal(barrier, 1, device_id=dev, device_id_type=MESH)
        pl.semaphore_wait(barrier, 5 + NW - 1)

    @pl.when(jnp.logical_not(worker))
    def _():
        pl.semaphore_wait(barrier, NW)

    def remote(src, dst, send, recv, dev):
        return pltpu.make_async_remote_copy(
            src_ref=src, dst_ref=dst, send_sem=send, recv_sem=recv, device_id=dev, device_id_type=MESH)

    h_out = [remote(h_buf.at[here], h_buf.at[here], hs_sem.at[k], hr_sem.at[0], (x, y, c, k)) for k in range(NW)]

    def send_rows():
        h_load.wait()
        for k, copy in enumerate(h_out):
            pl.when(z != k)(copy.start)

    e_out = [remote(e_buf.at[0], e_buf.at[1], es_sem.at[k], er_sem.at[0], dev)
             for k, dev in enumerate(others)]

    def work():
        low, high = pl.ds(0, HALF), pl.ds(HALF, HALF)
        low0, low1 = pl.ds(0, CHUNK), pl.ds(CHUNK, CHUNK)
        half = pl.ds(c * HALF, HALF)

        def a_copies(*where):
            return [remote(av.at[w], ao.at[w], a_sem.at[k], a_sem.at[2 + k], sib) for k, w in enumerate(where)]

        a_down = a_copies(low0, low1)
        a_up = a_copies(low, high)
        a_load.wait()

        @pl.when(c == 0)
        def _():
            for copy in a_up:
                copy.start()

        @pl.when(c == 1)
        def _():
            for copy in a_down:
                copy.start()
        send_rows()

        def rows(k, core=None):
            return pl.ds((c if core is None else core) * HALF + k * CHUNK, CHUNK)

        def subrows(k, core=None):
            return pl.ds((c if core is None else core) * HALF + k * PART, PART)

        def gather(buf, out_sem, in_sem, share_out, share_in, right, left):
            def copy(place, k, dev, n):
                there = buf.at[place, rows(k) if n < 4 else subrows(k)]
                return remote(there, there, out_sem.at[n], in_sem.at[n], dev)

            def share(place, k, n):
                there = buf.at[place, subrows(k) if 4 <= n < 8 else rows(k)]
                return remote(there, there, share_out.at[n], share_in.at[n], sib)

            def shared(place, k, n):
                there = buf.at[place, subrows(k, 1 - c) if 4 <= n < 8 else rows(k, 1 - c)]
                return remote(there, there, share_out.at[n], share_in.at[n], sib)

            return copy, share, shared

        y_copy, y_share, y_shared = gather(s_buf, ys_sem, yr_sem, yd_sem, ye_sem, right_y, left_y)
        y_out = [
            y_copy(y, 0, right_y, 0), y_copy(y, 1, left_y, 3),
            y_copy(y, 1, right_y, 1), y_copy(y, 0, left_y, 2),
        ]
        y_sh = {}

        def share_s(place, k, n):
            copy = y_share(place, k, n)
            copy.start()
            y_sh[n] = (copy, y_shared(place, k, n))

        @pl.when(c == 0)
        def _():
            a_down[0].wait_recv()
            s_buf[y, low0] = times(ao[low0], av[...])
            y_out[0].start()
            a_down[1].wait_recv()
            s_buf[y, low1] = times(ao[low1], av[...])

        @pl.when(c == 1)
        def _():
            for copy in a_up:
                copy.wait_recv()
            s_buf[y, high] = times(av[high], ao[...])
            y_out[0].start()

        for copy in y_out[1:]:
            copy.start()
        share_s(y, 0, 8)
        share_s(y, 1, 9)

        def relay(k, source, dev, n):
            for m in range(2):
                copy = y_copy(source, 2 * k + m, dev, n + m)
                copy.start()
                y_out.append(copy)

        y_copy(yl, 0, left_y, 0).wait_recv()
        relay(0, yl, right_y, 4)
        y_copy(yr, 1, right_y, 3).wait_recv()
        relay(1, yr, left_y, 6)
        share_s(yl, 0, 0)
        share_s(yr, 1, 3)
        y_copy(yl, 1, left_y, 1).wait_recv()
        share_s(yl, 1, 1)
        y_copy(yr, 0, left_y, 2).wait_recv()
        share_s(yr, 0, 2)
        for k, n in ((0, 4), (2, 6), (1, 5), (3, 7)):
            y_copy(yo, k, left_y, n).wait_recv()
            share_s(yo, k, n)

        for n in (8, 9, 0, 3, 1, 2):
            y_sh[n][1].wait_recv()

        ahead = x < NX - 1

        @pl.when(ahead & (y == 0))
        def _():
            z_buf[...] = times(s_buf[1], s_buf[0])

        @pl.when(ahead & (y == 1))
        def _():
            z_buf[...] = times(s_buf[2], times(s_buf[1], s_buf[0]))

        @pl.when(ahead & (y >= 2))
        def _():
            n_buf[...] = times(s_buf[3, half], s_buf[2])

        @pl.when(ahead & (y == 2))
        def _():
            n_buf[...] = times(n_buf[...], s_buf[1])

        def opposite_shared():
            for n in (4, 6, 5, 7):
                y_sh[n][1].wait_recv()

        pl.when(y != 1)(opposite_shared)

        @pl.when(ahead & (y == 0))
        def _():
            r_buf[x, half] = times(times(s_buf[3, half], s_buf[2]), z_buf[...])

        @pl.when(ahead & (y == 1))
        def _():
            r_buf[x, half] = times(s_buf[3, half], z_buf[...])

        @pl.when(ahead & (y == 2))
        def _():
            r_buf[x, half] = times(n_buf[...], s_buf[0])

        @pl.when(ahead & (y == 3))
        def _():
            r_buf[x, half] = times(times(n_buf[...], s_buf[1]), s_buf[0])

        x_copy, x_share, x_shared = gather(r_buf, xs_sem, xr_sem, xd_sem, xe_sem, right_x, left_x)

        to_right = x < 3
        first = x == 0
        last = x == 3
        x_out = []

        def when_start(cond, copy):
            @pl.when(cond)
            def _():
                copy.start()
            x_out.append((cond, copy))

        def when_recv(cond, copy):
            @pl.when(cond)
            def _():
                copy.wait_recv()

        when_start(to_right, x_copy(x, 0, right_x, 0))
        when_start(x < 2, x_copy(x, 1, left_x, 3))
        when_start(to_right, x_copy(x, 1, right_x, 1))
        when_start(first, x_copy(x, 0, left_x, 2))
        pl.when(y == 1)(opposite_shared)

        @pl.when(y == 1)
        def _():
            l_buf[...] = s_buf[0]

        @pl.when(y >= 2)
        def _():
            l_buf[...] = times(s_buf[1], s_buf[0])

        @pl.when((c == 1) & (y == 0))
        def _():
            l_buf[...] = ao[...]

        x_sh = {}

        def share_r(cond, place, k, n):
            copy = x_share(place, k, n)
            when_start(cond, copy)
            x_sh[n] = (cond, x_shared(place, k, n))

        from_left = x > 0
        opposite = x > 1
        when_recv(from_left, x_copy(xl, 0, left_x, 0))
        for m in range(2):
            when_start((x == 1) | (x == 2), x_copy(xl, m, right_x, 4 + m))
        when_recv(first | last, x_copy(xr, 1, right_x, 3))
        for m in range(2):
            when_start(first | last, x_copy(xr, 2 + m, left_x, 6 + m))
        share_r(from_left, xl, 0, 0)
        share_r(last, xr, 1, 3)

        @pl.when(y == 3)
        def _():
            l_buf[...] = times(s_buf[2], l_buf[...])

        @pl.when((c == 1) & (y > 0))
        def _():
            l_buf[...] = times(ao[...], l_buf[...])

        when_recv(from_left, x_copy(xl, 1, left_x, 1))
        share_r(from_left, xl, 1, 1)
        when_recv(last, x_copy(xr, 0, left_x, 2))
        share_r(last, xr, 0, 2)

        rest = h_buf.at[pl.ds(0, (NZ - 1) * HB)]
        remote(rest, rest, hs_sem.at[0], hr_sem.at[0], sib).wait_recv()
        inner = (y > 0) | (c > 0)

        @pl.when(jnp.logical_not(inner))
        def _():
            z_buf[...] = h_buf[...]

        @pl.when(inner)
        def _():
            z_buf[...] = times(l_buf[...], times(h_buf[...], l_buf[...]), TN)

        z_copy = remote(z_buf, zo_buf, zz_sem.at[0], zz_sem.at[1], sib)
        z_copy.start()

        part = z
        place = lax.broadcasted_iota(jnp.int32, (WIDE, D), 0)
        column = lax.broadcasted_iota(jnp.int32, (WIDE, D), 1)
        within = place & (PIECE - 1)
        wanted = part * (8 * ROWS) + (c * 4 + (place >> 4)) * ROWS + within
        u_buf[...] = jnp.where((within < ROWS) & (column == wanted), 1.0, 0.0).astype(F32)
        for n in (0, 3, 1, 2):
            when_recv(*x_sh[n])

        @pl.when((x == 1) | last)
        def _():
            u_buf[...] = times(u_buf[...], r_buf[0], NT)

        for k, n in ((0, 4), (2, 6), (1, 5), (3, 7)):
            when_recv(opposite, x_copy(xo, k, left_x, n))
            share_r(opposite, xo, k, n)
        for n in (4, 6, 5, 7):
            when_recv(*x_sh[n])

        @pl.when(x == 2)
        def _():
            u_buf[...] = times(u_buf[...], r_buf[0], NT)
        for k in (1, 2):
            @pl.when(x > k)
            def _(k=k):
                u_buf[...] = times(u_buf[...], r_buf[k], NT)
        z_copy.wait_recv()
        u_buf[...] = times(u_buf[...], z_buf[...] + zo_buf[...])

        t_out = []
        for q in range(4):
            yt, ct = c * 2 + q // 2, q % 2
            mine = (y == yt) & (c == ct)
            copy = remote(u_buf.at[pl.ds(q * PIECE, PIECE)], t_buf.at[y], ts_sem.at[q], tr_sem.at[y],
                          (x, yt, ct, z))

            @pl.when(mine)
            def _(q=q):
                t_buf[y] = u_buf[pl.ds(q * PIECE, PIECE)]

            @pl.when(jnp.logical_not(mine))
            def _(copy=copy):
                copy.start()
            t_out.append((jnp.logical_not(mine), copy))

        @pl.when(x >= 2)
        def _():
            l_buf[...] = times(r_buf[1], r_buf[0])

        @pl.when(x == 3)
        def _():
            l_buf[...] = times(r_buf[2], l_buf[...])
        holder = c == lax.div(y, 2)
        for k in range(NY):
            @pl.when(jnp.logical_not(holder & (y == k)))
            def _(k=k):
                remote(t_buf.at[k], t_buf.at[k], ts_sem.at[0], tr_sem.at[k], sib).wait_recv()
        v_buf[...] = (t_buf[0] + t_buf[1]) + (t_buf[2] + t_buf[3])

        @pl.when(x == 1)
        def _():
            v_buf[...] = times(v_buf[...], r_buf[0])

        @pl.when(x >= 2)
        def _():
            v_buf[...] = times(v_buf[...], l_buf[...])

        g_copy = remote(v_buf, g_buf.at[x], gs_sem.at[0], gr_sem.at[x], (z, y, c, z))

        @pl.when(jnp.logical_not(owner))
        def _():
            g_copy.start()

        @pl.when(owner)
        def _():
            total = v_buf[...]
            for k in (1, 3, 2):
                k = lax.rem(x + k, NX)
                remote(g_buf.at[k], g_buf.at[k], gs_sem.at[0], gr_sem.at[k], sib).wait_recv()
            for k in (1, 3, 2):
                total = total + g_buf[lax.rem(x + k, NX)]
            e_buf[0] = total[:ROWS]
            for k in (7, 8, 6, 9, 5, 10, 4, 11, 3, 12, 2, 13, 1, 14, 0):
                e_out[k].start()
            o_ref[...] = total[:ROWS]

        @pl.when(jnp.logical_not(owner))
        def _():
            g_copy.wait_send()

        @pl.when(c == 0)
        def _():
            for copy in a_up:
                copy.wait_send()

        @pl.when(c == 1)
        def _():
            for copy in a_down:
                copy.wait_send()
        z_copy.wait_send()
        for copy in y_out:
            copy.wait_send()
        for copy, _ in y_sh.values():
            copy.wait_send()
        for cond, copy in x_out + t_out:
            pl.when(cond)(copy.wait_send)

    @pl.when(worker)
    def _():
        work()

    @pl.when(jnp.logical_not(worker))
    def _():
        send_rows()

    @pl.when(owner)
    def _():
        for copy in e_out:
            copy.wait_send()

    @pl.when(jnp.logical_not(owner))
    def _():
        e_out[0].wait_recv()
        o_ref[...] = e_buf[1]

    for k, copy in enumerate(h_out):
        pl.when(z != k)(copy.wait_send)


def body(propagators, perturbation):
    full = pltpu.VMEM((D, D), F32)
    dma = pltpu.SemaphoreType.DMA
    return pl.pallas_call(
        kernel,
        out_shape=jax.ShapeDtypeStruct((ROWS, D), F32),
        in_specs=[pl.BlockSpec(memory_space=pltpu.HBM)] * 2,
        out_specs=pl.BlockSpec(memory_space=pltpu.VMEM),
        scratch_shapes=[
            full, full,
            pltpu.VMEM((NY, D, D), F32),
            pltpu.VMEM((NX, D, D), F32),
            full, full, full, full,
            pltpu.VMEM((WIDE, D), F32),
            pltpu.VMEM((NY, PIECE, D), F32),
            pltpu.VMEM((PIECE, D), F32),
            pltpu.VMEM((NX, PIECE, D), F32),
            pltpu.VMEM((HALF, D), F32),
            pltpu.VMEM((2, ROWS, D), F32),
            dma((2,)), dma((4,)),
            dma((8,)), dma((8,)), dma((10,)), dma((10,)),
            dma((8,)), dma((8,)), dma((8,)), dma((8,)),
            dma((NW,)), dma((1,)), dma((2,)),
            dma((4,)), dma((4,)),
            dma((1,)), dma((4,)),
            dma((NZ - 1,)), dma((1,)),
        ],
        compiler_params=pltpu.CompilerParams(
            collective_id=0, has_side_effects=True, vmem_limit_bytes=55192 * 1024),
        name="floquet",
    )(propagators, perturbation)


def solution(mesh):
    split = Mesh(mesh.devices.reshape(NX, NY, 2, NZ), AXES)
    tm = ("x", "y", "c")
    return jax.shard_map(
        body,
        mesh=split,
        in_specs=(P(tm, None, None), P(tm, "z", None)),
        out_specs=P(tm, None),
        check_vma=False,
    )
```

```python
import jax
import jax.numpy as jnp
from jax import lax
from jax.experimental import pallas as pl
from jax.experimental.pallas import tpu as pltpu
from jax.sharding import Mesh
from jax.sharding import PartitionSpec as P

AXES = ("x", "y", "c", "z")
MESH = pl.DeviceIdType.MESH
F32 = jnp.float32
BF16 = jnp.bfloat16
D = 384
HALF = D // 2
CHUNK = HALF // 2
PART = CHUNK // 2
NX = 4
NY = 4
NZ = 16
FIRST = 1
NW = 2
HB = D // NZ
ROWS = D // 32
UNIT = 16
SUB = NX // NW
PIECE = SUB * UNIT
WIDE = 4 * PIECE
NN = ((1,), (0,))
NT = ((1,), (1,))
TN = ((0,), (0,))


def parts(value):
    high = value.astype(BF16)
    return high, (value - high.astype(F32)).astype(BF16)


def bdot(left, right, dims):
    return lax.dot_general(left, right, (dims, ((), ())), preferred_element_type=F32)


def times(left, right, dims=NN):
    lh, ll = parts(left)
    rh, rl = parts(right)
    if dims is TN:
        return bdot(lh, rh, dims) + (bdot(ll, rh, dims) + bdot(lh, rl, dims))
    n = left.shape[0]
    both = bdot(jnp.concatenate([lh, ll], axis=0), rh, dims)
    return both[:n] + (both[n:] + bdot(lh, rl, dims))


def kernel(a_hbm, h_hbm, o_ref, av, ao, s_buf, r_buf, h_buf, l_buf, z_buf, zo_buf, u_buf, t_buf, v_buf, g_buf, n_buf,
           e_buf, w_buf, f_buf, in_sem, a_sem, ys_sem, yr_sem, yd_sem, ye_sem, xs_sem, xr_sem, xd_sem, xe_sem,
           hs_sem, hr_sem, zz_sem, ts_sem, tr_sem, gs_sem, gr_sem, es_sem, er_sem):
    x, y, c, z = (lax.axis_index(a) for a in AXES)
    worker = (z >= FIRST) & (z < FIRST + NW)
    owner = z == FIRST + lax.div(x, SUB)
    lot = (z - FIRST) * SUB
    here = pl.ds(z * HB, HB)
    a_load = pltpu.make_async_copy(a_hbm.at[0], av, in_sem.at[0])
    h_load = pltpu.make_async_copy(h_hbm.at[0], h_buf.at[here], in_sem.at[1])
    pl.when(worker)(a_load.start)
    h_load.start()
    xr, xl, xo = (lax.rem(x + k, NX) for k in (1, 3, 2))
    yr, yl, yo = (lax.rem(y + k, NY) for k in (1, 3, 2))
    others = [(x, y, c, lax.rem(z + k, NZ)) for k in range(1, NZ)]
    sib = (x, y, 1 - c, z)
    right_y, left_y = (x, yr, c, z), (x, yl, c, z)
    right_x, left_x = (xr, y, c, z), (xl, y, c, z)

    barrier = pltpu.get_barrier_semaphore()

    @pl.when(worker)
    def _():
        for dev in [sib, right_y, left_y, right_x, left_x] + others:
            pl.semaphore_signal(barrier, 1, device_id=dev, device_id_type=MESH)
        pl.semaphore_wait(barrier, 5 + NW - 1)

    @pl.when(jnp.logical_not(worker))
    def _():
        pl.semaphore_wait(barrier, NW)

    def remote(src, dst, send, recv, dev):
        return pltpu.make_async_remote_copy(
            src_ref=src, dst_ref=dst, send_sem=send, recv_sem=recv, device_id=dev, device_id_type=MESH)

    h_out = [remote(h_buf.at[here], h_buf.at[here], hs_sem.at[k], hr_sem.at[0], (x, y, c, FIRST + k))
             for k in range(NW)]

    def send_rows():
        h_load.wait()
        for k, copy in enumerate(h_out):
            pl.when(z != FIRST + k)(copy.start)

    e_out = [remote(e_buf.at[0], e_buf.at[1], es_sem.at[k], er_sem.at[0], dev)
             for k, dev in enumerate(others)]

    def work():
        low, high = pl.ds(0, HALF), pl.ds(HALF, HALF)
        low0, low1 = pl.ds(0, CHUNK), pl.ds(CHUNK, CHUNK)
        half = pl.ds(c * HALF, HALF)

        def a_copies(*where):
            return [remote(av.at[w], ao.at[w], a_sem.at[k], a_sem.at[2 + k], sib) for k, w in enumerate(where)]

        a_down = a_copies(low0, low1)
        a_up = a_copies(low, high)
        a_load.wait()

        @pl.when(c == 0)
        def _():
            for copy in a_up:
                copy.start()

        @pl.when(c == 1)
        def _():
            for copy in a_down:
                copy.start()
        send_rows()

        def rows(k, core=None):
            return pl.ds((c if core is None else core) * HALF + k * CHUNK, CHUNK)

        def subrows(k, core=None):
            return pl.ds((c if core is None else core) * HALF + k * PART, PART)

        def gather(buf, out_sem, in_sem, share_out, share_in, right, left):
            def copy(place, k, dev, n):
                there = buf.at[place, rows(k) if n < 4 else subrows(k)]
                return remote(there, there, out_sem.at[n], in_sem.at[n], dev)

            def share(place, k, n):
                there = buf.at[place, subrows(k) if 4 <= n < 8 else rows(k)]
                return remote(there, there, share_out.at[n], share_in.at[n], sib)

            def shared(place, k, n):
                there = buf.at[place, subrows(k, 1 - c) if 4 <= n < 8 else rows(k, 1 - c)]
                return remote(there, there, share_out.at[n], share_in.at[n], sib)

            return copy, share, shared

        y_copy, y_share, y_shared = gather(s_buf, ys_sem, yr_sem, yd_sem, ye_sem, right_y, left_y)
        y_out = [
            y_copy(y, 0, right_y, 0), y_copy(y, 1, left_y, 3),
            y_copy(y, 1, right_y, 1), y_copy(y, 0, left_y, 2),
        ]
        y_sh = {}

        def share_s(place, k, n):
            copy = y_share(place, k, n)
            copy.start()
            y_sh[n] = (copy, y_shared(place, k, n))

        @pl.when(c == 0)
        def _():
            a_down[0].wait_recv()
            s_buf[y, low0] = times(ao[low0], av[...])
            y_out[0].start()
            a_down[1].wait_recv()
            s_buf[y, low1] = times(ao[low1], av[...])

        @pl.when(c == 1)
        def _():
            for copy in a_up:
                copy.wait_recv()
            s_buf[y, high] = times(av[high], ao[...])
            y_out[0].start()

        for copy in y_out[1:]:
            copy.start()
        share_s(y, 0, 8)
        share_s(y, 1, 9)

        def relay(k, source, dev, n):
            for m in range(2):
                copy = y_copy(source, 2 * k + m, dev, n + m)
                copy.start()
                y_out.append(copy)

        y_copy(yl, 0, left_y, 0).wait_recv()
        relay(0, yl, right_y, 4)
        y_copy(yr, 1, right_y, 3).wait_recv()
        relay(1, yr, left_y, 6)
        share_s(yl, 0, 0)
        share_s(yr, 1, 3)
        y_copy(yl, 1, left_y, 1).wait_recv()
        share_s(yl, 1, 1)
        y_copy(yr, 0, left_y, 2).wait_recv()
        share_s(yr, 0, 2)
        for k, n in ((0, 4), (2, 6), (1, 5), (3, 7)):
            y_copy(yo, k, left_y, n).wait_recv()
            share_s(yo, k, n)

        for n in (8, 9, 0, 3, 1, 2):
            y_sh[n][1].wait_recv()

        ahead = x < NX - 1

        @pl.when(ahead & (y == 0))
        def _():
            z_buf[...] = times(s_buf[1], s_buf[0])

        @pl.when(ahead & (y == 1))
        def _():
            z_buf[...] = times(s_buf[2], times(s_buf[1], s_buf[0]))

        @pl.when(ahead & (y >= 2))
        def _():
            n_buf[...] = times(s_buf[3, half], s_buf[2])

        @pl.when(ahead & (y == 2))
        def _():
            n_buf[...] = times(n_buf[...], s_buf[1])

        def opposite_shared():
            for n in (4, 6, 5, 7):
                y_sh[n][1].wait_recv()

        pl.when(y != 1)(opposite_shared)

        @pl.when(ahead & (y == 0))
        def _():
            r_buf[x, half] = times(times(s_buf[3, half], s_buf[2]), z_buf[...])

        @pl.when(ahead & (y == 1))
        def _():
            r_buf[x, half] = times(s_buf[3, half], z_buf[...])

        @pl.when(ahead & (y == 2))
        def _():
            r_buf[x, half] = times(n_buf[...], s_buf[0])

        @pl.when(ahead & (y == 3))
        def _():
            r_buf[x, half] = times(times(n_buf[...], s_buf[1]), s_buf[0])

        x_copy, x_share, x_shared = gather(r_buf, xs_sem, xr_sem, xd_sem, xe_sem, right_x, left_x)

        to_right = x < 3
        first = x == 0
        last = x == 3
        x_out = []

        def when_start(cond, copy):
            @pl.when(cond)
            def _():
                copy.start()
            x_out.append((cond, copy))

        def when_recv(cond, copy):
            @pl.when(cond)
            def _():
                copy.wait_recv()

        when_start(to_right, x_copy(x, 0, right_x, 0))
        when_start(x < 2, x_copy(x, 1, left_x, 3))
        when_start(to_right, x_copy(x, 1, right_x, 1))
        when_start(first, x_copy(x, 0, left_x, 2))
        pl.when(y == 1)(opposite_shared)

        @pl.when(y == 1)
        def _():
            l_buf[...] = s_buf[0]

        @pl.when(y >= 2)
        def _():
            l_buf[...] = times(s_buf[1], s_buf[0])

        @pl.when((c == 1) & (y == 0))
        def _():
            l_buf[...] = ao[...]

        @pl.when(y == 3)
        def _():
            l_buf[...] = times(s_buf[2], l_buf[...])

        @pl.when((c == 1) & (y > 0))
        def _():
            l_buf[...] = times(ao[...], l_buf[...])

        x_sh = {}

        def share_r(cond, place, k, n):
            copy = x_share(place, k, n)
            when_start(cond, copy)
            x_sh[n] = (cond, x_shared(place, k, n))

        from_left = x > 0
        opposite = x > 1
        when_recv(from_left, x_copy(xl, 0, left_x, 0))
        for m in range(2):
            when_start((x == 1) | (x == 2), x_copy(xl, m, right_x, 4 + m))
        when_recv(first | last, x_copy(xr, 1, right_x, 3))
        for m in range(2):
            when_start(first | last, x_copy(xr, 2 + m, left_x, 6 + m))
        share_r(from_left, xl, 0, 0)
        share_r(last, xr, 1, 3)

        rest = h_buf.at[pl.ds(0, (NZ - 1) * HB)]
        remote(rest, rest, hs_sem.at[0], hr_sem.at[0], sib).wait_recv()
        inner = (y > 0) | (c > 0)

        @pl.when(jnp.logical_not(inner))
        def _():
            z_buf[...] = h_buf[...]

        @pl.when(inner)
        def _():
            z_buf[...] = times(l_buf[...], times(h_buf[...], l_buf[...]), TN)

        z_copy = remote(z_buf, zo_buf, zz_sem.at[0], zz_sem.at[1], sib)
        z_copy.start()

        when_recv(from_left, x_copy(xl, 1, left_x, 1))
        share_r(from_left, xl, 1, 1)
        when_recv(last, x_copy(xr, 0, left_x, 2))
        share_r(last, xr, 0, 2)

        place = lax.broadcasted_iota(jnp.int32, (WIDE, D), 0)
        column = lax.broadcasted_iota(jnp.int32, (WIDE, D), 1)
        within = lax.rem(place, UNIT)
        block = lot + lax.rem(lax.div(place, UNIT), SUB)
        wanted = block * (8 * ROWS) + (lax.div(place, PIECE) * 2 + c) * ROWS + within
        u_buf[...] = jnp.where((within < ROWS) & (column == wanted), 1.0, 0.0).astype(F32)
        for n in (0, 3, 1, 2):
            when_recv(*x_sh[n])

        @pl.when((x == 1) | last)
        def _():
            u_buf[...] = times(u_buf[...], r_buf[0], NT)

        for k, n in ((0, 4), (2, 6), (1, 5), (3, 7)):
            when_recv(opposite, x_copy(xo, k, left_x, n))
            share_r(opposite, xo, k, n)

        z_copy.wait_recv()
        z_copy.wait_send()
        z_buf[...] = z_buf[...] + zo_buf[...]

        @pl.when(x == 2)
        def _():
            z_buf[...] = times(r_buf[1], z_buf[...], TN)

        @pl.when(x == 3)
        def _():
            z_buf[...] = times(r_buf[2], z_buf[...], TN)
        for n in (4, 6, 5, 7):
            when_recv(*x_sh[n])

        @pl.when(x == 2)
        def _():
            u_buf[...] = times(u_buf[...], r_buf[0], NT)

        @pl.when(x == 3)
        def _():
            u_buf[...] = times(u_buf[...], r_buf[1], NT)
        u_buf[...] = times(u_buf[...], z_buf[...])

        t_out = []
        for q in range(4):
            for k in range(SUB):
                w_buf[q, k] = u_buf[pl.ds(q * PIECE + k * UNIT, ROWS)]
        for q in range(4):
            mine = y == q
            copy = remote(w_buf.at[q], t_buf.at[y], ts_sem.at[q], tr_sem.at[y], (x, q, c, z))

            @pl.when(mine)
            def _(q=q):
                t_buf[y] = w_buf[q]

            @pl.when(jnp.logical_not(mine))
            def _(copy=copy):
                copy.start()
            t_out.append((jnp.logical_not(mine), copy))

        v_buf[...] = jnp.zeros((PIECE, D), F32)

        @pl.when(x >= 2)
        def _():
            l_buf[...] = times(r_buf[1], r_buf[0])

        @pl.when(x == 3)
        def _():
            l_buf[...] = times(r_buf[2], l_buf[...])
        for k in range(NY):
            @pl.when(y != k)
            def _(k=k):
                remote(t_buf.at[k], t_buf.at[k], ts_sem.at[0], tr_sem.at[k], sib).wait_recv()
        for k in range(SUB):
            v_buf[pl.ds(k * UNIT, ROWS)] = (t_buf[0, k] + t_buf[1, k]) + (t_buf[2, k] + t_buf[3, k])
        value = v_buf[...]

        def place_pieces(value):
            for k in range(SUB):
                f_buf[k] = value[k * UNIT:k * UNIT + ROWS]

        @pl.when(x == 0)
        def _():
            place_pieces(value)

        @pl.when(x == 1)
        def _():
            place_pieces(times(value, r_buf[0]))

        @pl.when(x >= 2)
        def _():
            place_pieces(times(value, l_buf[...]))

        for k in range(SUB):
            there = lot + k
            copy = remote(f_buf.at[k], g_buf.at[x], gs_sem.at[k], gr_sem.at[x], (there, y, c, z))
            pl.when(x != there)(copy.start)
            t_out.append((x != there, copy))

        @pl.when(owner)
        def _():
            total = f_buf[x - lot]
            for k in (1, 3, 2):
                k = lax.rem(x + k, NX)
                remote(g_buf.at[k], g_buf.at[k], gs_sem.at[0], gr_sem.at[k], sib).wait_recv()
            for k in (1, 3, 2):
                total = total + g_buf[lax.rem(x + k, NX)]
            e_buf[0] = total
            for k in (7, 8, 6, 9, 5, 10, 4, 11, 3, 12, 2, 13, 1, 14, 0):
                e_out[k].start()
            o_ref[...] = total

        @pl.when(c == 0)
        def _():
            for copy in a_up:
                copy.wait_send()

        @pl.when(c == 1)
        def _():
            for copy in a_down:
                copy.wait_send()
        for copy in y_out:
            copy.wait_send()
        for copy, _ in y_sh.values():
            copy.wait_send()
        for cond, copy in x_out + t_out:
            pl.when(cond)(copy.wait_send)

    @pl.when(worker)
    def _():
        work()

    @pl.when(jnp.logical_not(worker))
    def _():
        send_rows()

    @pl.when(owner)
    def _():
        for copy in e_out:
            copy.wait_send()

    @pl.when(jnp.logical_not(owner))
    def _():
        e_out[0].wait_recv()
        o_ref[...] = e_buf[1]

    for k, copy in enumerate(h_out):
        pl.when(z != FIRST + k)(copy.wait_send)


def body(propagators, perturbation):
    full = pltpu.VMEM((D, D), F32)
    dma = pltpu.SemaphoreType.DMA
    return pl.pallas_call(
        kernel,
        out_shape=jax.ShapeDtypeStruct((ROWS, D), F32),
        in_specs=[pl.BlockSpec(memory_space=pltpu.HBM)] * 2,
        out_specs=pl.BlockSpec(memory_space=pltpu.VMEM),
        scratch_shapes=[
            full, full,
            pltpu.VMEM((NY, D, D), F32),
            pltpu.VMEM((NX, D, D), F32),
            full, full, full, full,
            pltpu.VMEM((WIDE, D), F32),
            pltpu.VMEM((NY, SUB, ROWS, D), F32),
            pltpu.VMEM((PIECE, D), F32),
            pltpu.VMEM((NX, ROWS, D), F32),
            pltpu.VMEM((HALF, D), F32),
            pltpu.VMEM((2, ROWS, D), F32),
            pltpu.VMEM((4, SUB, ROWS, D), F32),
            pltpu.VMEM((SUB, ROWS, D), F32),
            dma((2,)), dma((4,)),
            dma((8,)), dma((8,)), dma((10,)), dma((10,)),
            dma((8,)), dma((8,)), dma((8,)), dma((8,)),
            dma((NW,)), dma((1,)), dma((2,)),
            dma((4,)), dma((4,)),
            dma((SUB,)), dma((4,)),
            dma((NZ - 1,)), dma((1,)),
        ],
        compiler_params=pltpu.CompilerParams(
            collective_id=0, has_side_effects=True, vmem_limit_bytes=55192 * 1024),
        name="floquet",
    )(propagators, perturbation)


def solution(mesh):
    split = Mesh(mesh.devices.reshape(NX, NY, 2, NZ), AXES)
    tm = ("x", "y", "c")
    return jax.shard_map(
        body,
        mesh=split,
        in_specs=(P(tm, None, None), P(tm, "z", None)),
        out_specs=P(tm, None),
        check_vma=False,
    )
```

```python
import jax
import jax.numpy as jnp
from jax import lax
from jax.experimental import pallas as pl
from jax.experimental.pallas import tpu as pltpu
from jax.sharding import Mesh
from jax.sharding import PartitionSpec as P

AXES = ("x", "y", "c", "z")
MESH = pl.DeviceIdType.MESH
F32 = jnp.float32
BF16 = jnp.bfloat16
D = 384
HALF = D // 2
CHUNK = HALF // 2
PART = CHUNK // 2
NX = 4
NY = 4
NZ = 16
FIRST = 1
NW = 2
HB = D // NZ
ROWS = D // 32
UNIT = 16
SUB = NX // NW
PIECE = SUB * UNIT
WIDE = 4 * PIECE
NN = ((1,), (0,))
NT = ((1,), (1,))
TN = ((0,), (0,))


def parts(value):
    high = value.astype(BF16)
    return high, (value - high.astype(F32)).astype(BF16)


def bdot(left, right, dims):
    return lax.dot_general(left, right, (dims, ((), ())), preferred_element_type=F32)


def times(left, right, dims=NN):
    lh, ll = parts(left)
    rh, rl = parts(right)
    if dims is TN:
        return bdot(lh, rh, dims) + (bdot(ll, rh, dims) + bdot(lh, rl, dims))
    n = left.shape[0]
    both = bdot(jnp.concatenate([lh, ll], axis=0), rh, dims)
    return both[:n] + (both[n:] + bdot(lh, rl, dims))


def kernel(a_hbm, h_hbm, o_ref, av, ao, s_buf, r_buf, h_buf, l_buf, z_buf, zo_buf, u_buf, t_buf, v_buf, g_buf, n_buf,
           e_buf, w_buf, f_buf, in_sem, a_sem, ys_sem, yr_sem, yd_sem, ye_sem, xs_sem, xr_sem, xd_sem, xe_sem,
           hs_sem, hr_sem, zz_sem, ts_sem, tr_sem, gs_sem, gr_sem, es_sem, er_sem):
    x, y, c, z = (lax.axis_index(a) for a in AXES)
    worker = (z >= FIRST) & (z < FIRST + NW)
    owner = z == FIRST + lax.div(x, SUB)
    lot = (z - FIRST) * SUB
    here = pl.ds(z * HB, HB)
    a_load = pltpu.make_async_copy(a_hbm.at[0], av, in_sem.at[0])
    h_load = pltpu.make_async_copy(h_hbm.at[0], h_buf.at[here], in_sem.at[1])
    pl.when(worker)(a_load.start)
    h_load.start()
    xr, xl, xo = (lax.rem(x + k, NX) for k in (1, 3, 2))
    yr, yl, yo = (lax.rem(y + k, NY) for k in (1, 3, 2))
    others = [(x, y, c, lax.rem(z + k, NZ)) for k in range(1, NZ)]
    sib = (x, y, 1 - c, z)
    right_y, left_y = (x, yr, c, z), (x, yl, c, z)
    right_x, left_x = (xr, y, c, z), (xl, y, c, z)

    barrier = pltpu.get_barrier_semaphore()

    @pl.when(worker)
    def _():
        for dev in [sib, right_y, left_y, right_x, left_x] + others:
            pl.semaphore_signal(barrier, 1, device_id=dev, device_id_type=MESH)
        pl.semaphore_wait(barrier, 5 + NW - 1)

    @pl.when(jnp.logical_not(worker))
    def _():
        pl.semaphore_wait(barrier, NW)

    def remote(src, dst, send, recv, dev):
        return pltpu.make_async_remote_copy(
            src_ref=src, dst_ref=dst, send_sem=send, recv_sem=recv, device_id=dev, device_id_type=MESH)

    h_out = [remote(h_buf.at[here], h_buf.at[here], hs_sem.at[k], hr_sem.at[0], (x, y, c, FIRST + k))
             for k in range(NW)]

    def send_rows():
        h_load.wait()
        for k, copy in enumerate(h_out):
            pl.when(z != FIRST + k)(copy.start)

    e_out = [remote(e_buf.at[0], e_buf.at[1], es_sem.at[k], er_sem.at[0], dev)
             for k, dev in enumerate(others)]

    def work():
        low, high = pl.ds(0, HALF), pl.ds(HALF, HALF)
        low0, low1 = pl.ds(0, CHUNK), pl.ds(CHUNK, CHUNK)
        half = pl.ds(c * HALF, HALF)

        def a_copies(*where):
            return [remote(av.at[w], ao.at[w], a_sem.at[k], a_sem.at[2 + k], sib) for k, w in enumerate(where)]

        a_down = a_copies(low0, low1)
        a_up = a_copies(low, high)
        a_load.wait()

        @pl.when(c == 0)
        def _():
            for copy in a_up:
                copy.start()

        @pl.when(c == 1)
        def _():
            for copy in a_down:
                copy.start()
        send_rows()

        def rows(k, core=None):
            return pl.ds((c if core is None else core) * HALF + k * CHUNK, CHUNK)

        def subrows(k, core=None):
            return pl.ds((c if core is None else core) * HALF + k * PART, PART)

        def gather(buf, out_sem, in_sem, share_out, share_in, right, left):
            def copy(place, k, dev, n):
                there = buf.at[place, rows(k) if n < 4 else subrows(k)]
                return remote(there, there, out_sem.at[n], in_sem.at[n], dev)

            def share(place, k, n):
                there = buf.at[place, subrows(k) if 4 <= n < 8 else rows(k)]
                return remote(there, there, share_out.at[n], share_in.at[n], sib)

            def shared(place, k, n):
                there = buf.at[place, subrows(k, 1 - c) if 4 <= n < 8 else rows(k, 1 - c)]
                return remote(there, there, share_out.at[n], share_in.at[n], sib)

            return copy, share, shared

        y_copy, y_share, y_shared = gather(s_buf, ys_sem, yr_sem, yd_sem, ye_sem, right_y, left_y)
        y_out = [
            y_copy(y, 0, right_y, 0), y_copy(y, 1, left_y, 3),
            y_copy(y, 1, right_y, 1), y_copy(y, 0, left_y, 2),
        ]
        y_sh = {}

        def share_s(place, k, n):
            copy = y_share(place, k, n)
            copy.start()
            y_sh[n] = (copy, y_shared(place, k, n))

        @pl.when(c == 0)
        def _():
            a_down[0].wait_recv()
            s_buf[y, low0] = times(ao[low0], av[...])
            y_out[0].start()
            a_down[1].wait_recv()
            s_buf[y, low1] = times(ao[low1], av[...])

        @pl.when(c == 1)
        def _():
            for copy in a_up:
                copy.wait_recv()
            s_buf[y, high] = times(av[high], ao[...])
            y_out[0].start()

        for copy in y_out[1:]:
            copy.start()
        share_s(y, 0, 8)
        share_s(y, 1, 9)

        def relay(k, source, dev, n):
            for m in range(2):
                copy = y_copy(source, 2 * k + m, dev, n + m)
                copy.start()
                y_out.append(copy)

        y_copy(yl, 0, left_y, 0).wait_recv()
        relay(0, yl, right_y, 4)
        y_copy(yr, 1, right_y, 3).wait_recv()
        relay(1, yr, left_y, 6)
        share_s(yl, 0, 0)
        share_s(yr, 1, 3)
        y_copy(yl, 1, left_y, 1).wait_recv()
        share_s(yl, 1, 1)
        y_copy(yr, 0, left_y, 2).wait_recv()
        share_s(yr, 0, 2)
        for k, n in ((0, 4), (2, 6), (1, 5), (3, 7)):
            y_copy(yo, k, left_y, n).wait_recv()
            share_s(yo, k, n)

        for n in (8, 9, 0, 3, 1, 2):
            y_sh[n][1].wait_recv()

        ahead = x < NX - 1

        @pl.when(ahead & (y == 0))
        def _():
            z_buf[...] = times(s_buf[1], s_buf[0])

        @pl.when(ahead & (y == 1))
        def _():
            z_buf[...] = times(s_buf[2], times(s_buf[1], s_buf[0]))

        @pl.when(ahead & (y >= 2))
        def _():
            n_buf[...] = times(s_buf[3, half], s_buf[2])

        @pl.when(ahead & (y == 2))
        def _():
            n_buf[...] = times(n_buf[...], s_buf[1])

        def opposite_shared():
            for n in (4, 6, 5, 7):
                y_sh[n][1].wait_recv()

        pl.when(y != 1)(opposite_shared)

        @pl.when(ahead & (y == 0))
        def _():
            r_buf[x, half] = times(times(s_buf[3, half], s_buf[2]), z_buf[...])

        @pl.when(ahead & (y == 1))
        def _():
            r_buf[x, half] = times(s_buf[3, half], z_buf[...])

        @pl.when(ahead & (y == 2))
        def _():
            r_buf[x, half] = times(n_buf[...], s_buf[0])

        @pl.when(ahead & (y == 3))
        def _():
            r_buf[x, half] = times(times(n_buf[...], s_buf[1]), s_buf[0])

        x_copy, x_share, x_shared = gather(r_buf, xs_sem, xr_sem, xd_sem, xe_sem, right_x, left_x)

        to_right = x < 3
        first = x == 0
        last = x == 3
        x_out = []

        def when_start(cond, copy):
            @pl.when(cond)
            def _():
                copy.start()
            x_out.append((cond, copy))

        def when_recv(cond, copy):
            @pl.when(cond)
            def _():
                copy.wait_recv()

        when_start(to_right, x_copy(x, 0, right_x, 0))
        when_start(x < 2, x_copy(x, 1, left_x, 3))
        when_start(to_right, x_copy(x, 1, right_x, 1))
        when_start(first, x_copy(x, 0, left_x, 2))
        pl.when(y == 1)(opposite_shared)

        @pl.when(y == 1)
        def _():
            l_buf[...] = s_buf[0]

        @pl.when(y >= 2)
        def _():
            l_buf[...] = times(s_buf[1], s_buf[0])

        @pl.when((c == 1) & (y == 0))
        def _():
            l_buf[...] = ao[...]

        @pl.when(y == 3)
        def _():
            l_buf[...] = times(s_buf[2], l_buf[...])

        @pl.when((c == 1) & (y > 0))
        def _():
            l_buf[...] = times(ao[...], l_buf[...])

        x_sh = {}

        def share_r(cond, place, k, n):
            copy = x_share(place, k, n)
            when_start(cond, copy)
            x_sh[n] = (cond, x_shared(place, k, n))

        from_left = x > 0
        opposite = x > 1
        when_recv(from_left, x_copy(xl, 0, left_x, 0))
        for m in range(2):
            when_start((x == 1) | (x == 2), x_copy(xl, m, right_x, 4 + m))
        when_recv(first | last, x_copy(xr, 1, right_x, 3))
        for m in range(2):
            when_start(first | last, x_copy(xr, 2 + m, left_x, 6 + m))
        share_r(from_left, xl, 0, 0)
        share_r(last, xr, 1, 3)

        rest = h_buf.at[pl.ds(0, (NZ - 1) * HB)]
        remote(rest, rest, hs_sem.at[0], hr_sem.at[0], sib).wait_recv()
        inner = (y > 0) | (c > 0)

        @pl.when(jnp.logical_not(inner))
        def _():
            z_buf[...] = h_buf[...]

        @pl.when(inner)
        def _():
            z_buf[...] = times(l_buf[...], times(h_buf[...], l_buf[...]), TN)

        z_copy = remote(z_buf, zo_buf, zz_sem.at[0], zz_sem.at[1], sib)
        z_copy.start()

        when_recv(from_left, x_copy(xl, 1, left_x, 1))
        share_r(from_left, xl, 1, 1)
        when_recv(last, x_copy(xr, 0, left_x, 2))
        share_r(last, xr, 0, 2)

        place = lax.broadcasted_iota(jnp.int32, (WIDE, D), 0)
        column = lax.broadcasted_iota(jnp.int32, (WIDE, D), 1)
        within = lax.rem(place, UNIT)
        block = lot + lax.rem(lax.div(place, UNIT), SUB)
        wanted = block * (8 * ROWS) + (lax.div(place, PIECE) * 2 + c) * ROWS + within
        u_buf[...] = jnp.where((within < ROWS) & (column == wanted), 1.0, 0.0).astype(F32)
        for n in (0, 3, 1, 2):
            when_recv(*x_sh[n])

        @pl.when((x == 1) | last)
        def _():
            u_buf[...] = times(u_buf[...], r_buf[0], NT)

        for k, n in ((0, 4), (2, 6), (1, 5), (3, 7)):
            when_recv(opposite, x_copy(xo, k, left_x, n))
            share_r(opposite, xo, k, n)

        z_copy.wait_recv()
        z_copy.wait_send()
        z_buf[...] = z_buf[...] + zo_buf[...]

        @pl.when(x == 2)
        def _():
            z_buf[...] = times(r_buf[1], z_buf[...], TN)

        @pl.when(x == 3)
        def _():
            z_buf[...] = times(r_buf[2], z_buf[...], TN)
        for n in (4, 6, 5, 7):
            when_recv(*x_sh[n])

        @pl.when(x == 2)
        def _():
            u_buf[...] = times(u_buf[...], r_buf[0], NT)

        @pl.when(x == 3)
        def _():
            u_buf[...] = times(u_buf[...], r_buf[1], NT)
        u_buf[...] = times(u_buf[...], z_buf[...])

        t_out = []
        for q in range(4):
            for k in range(SUB):
                w_buf[q, k] = u_buf[pl.ds(q * PIECE + k * UNIT, ROWS)]
        for q in range(4):
            mine = y == q
            copy = remote(w_buf.at[q], t_buf.at[y], ts_sem.at[q], tr_sem.at[y], (x, q, c, z))

            @pl.when(mine)
            def _(q=q):
                t_buf[y] = w_buf[q]

            @pl.when(jnp.logical_not(mine))
            def _(copy=copy):
                copy.start()
            t_out.append((jnp.logical_not(mine), copy))

        v_buf[...] = jnp.zeros((PIECE, D), F32)

        @pl.when(x >= 2)
        def _():
            l_buf[...] = times(r_buf[1], r_buf[0])

        @pl.when(x == 3)
        def _():
            l_buf[...] = times(r_buf[2], l_buf[...])
        for k in range(NY):
            @pl.when(y != k)
            def _(k=k):
                remote(t_buf.at[k], t_buf.at[k], ts_sem.at[0], tr_sem.at[k], sib).wait_recv()
        for k in range(SUB):
            v_buf[pl.ds(k * UNIT, ROWS)] = (t_buf[0, k] + t_buf[1, k]) + (t_buf[2, k] + t_buf[3, k])
        value = v_buf[...]

        def place_pieces(value):
            for k in range(SUB):
                f_buf[k] = value[k * UNIT:k * UNIT + ROWS]

        @pl.when(x == 0)
        def _():
            place_pieces(value)

        @pl.when(x == 1)
        def _():
            place_pieces(times(value, r_buf[0]))

        @pl.when(x >= 2)
        def _():
            place_pieces(times(value, l_buf[...]))

        for k in range(SUB):
            there = lot + k
            copy = remote(f_buf.at[k], g_buf.at[x], gs_sem.at[k], gr_sem.at[x], (there, y, c, z))
            pl.when(x != there)(copy.start)
            t_out.append((x != there, copy))

        @pl.when(owner)
        def _():
            total = f_buf[x - lot]
            for k in (1, 3, 2):
                k = lax.rem(x + k, NX)
                remote(g_buf.at[k], g_buf.at[k], gs_sem.at[0], gr_sem.at[k], sib).wait_recv()
            for k in (1, 3, 2):
                total = total + g_buf[lax.rem(x + k, NX)]
            e_buf[0] = total
            for k in (14, 0, 13, 1, 2, 3, 4, 5, 12, 11, 10, 6, 7, 8, 9):
                e_out[k].start()
            o_ref[...] = total

        @pl.when(c == 0)
        def _():
            for copy in a_up:
                copy.wait_send()

        @pl.when(c == 1)
        def _():
            for copy in a_down:
                copy.wait_send()
        for copy in y_out:
            copy.wait_send()
        for copy, _ in y_sh.values():
            copy.wait_send()
        for cond, copy in x_out + t_out:
            pl.when(cond)(copy.wait_send)

    @pl.when(worker)
    def _():
        work()

    @pl.when(jnp.logical_not(worker))
    def _():
        send_rows()

    @pl.when(owner)
    def _():
        for copy in e_out:
            copy.wait_send()

    @pl.when(jnp.logical_not(owner))
    def _():
        e_out[0].wait_recv()
        o_ref[...] = e_buf[1]

    for k, copy in enumerate(h_out):
        pl.when(z != FIRST + k)(copy.wait_send)


def body(propagators, perturbation):
    full = pltpu.VMEM((D, D), F32)
    dma = pltpu.SemaphoreType.DMA
    return pl.pallas_call(
        kernel,
        out_shape=jax.ShapeDtypeStruct((ROWS, D), F32),
        in_specs=[pl.BlockSpec(memory_space=pltpu.HBM)] * 2,
        out_specs=pl.BlockSpec(memory_space=pltpu.VMEM),
        scratch_shapes=[
            full, full,
            pltpu.VMEM((NY, D, D), F32),
            pltpu.VMEM((NX, D, D), F32),
            full, full, full, full,
            pltpu.VMEM((WIDE, D), F32),
            pltpu.VMEM((NY, SUB, ROWS, D), F32),
            pltpu.VMEM((PIECE, D), F32),
            pltpu.VMEM((NX, ROWS, D), F32),
            pltpu.VMEM((HALF, D), F32),
            pltpu.VMEM((2, ROWS, D), F32),
            pltpu.VMEM((4, SUB, ROWS, D), F32),
            pltpu.VMEM((SUB, ROWS, D), F32),
            dma((2,)), dma((4,)),
            dma((8,)), dma((8,)), dma((10,)), dma((10,)),
            dma((8,)), dma((8,)), dma((8,)), dma((8,)),
            dma((NW,)), dma((1,)), dma((2,)),
            dma((4,)), dma((4,)),
            dma((SUB,)), dma((4,)),
            dma((NZ - 1,)), dma((1,)),
        ],
        compiler_params=pltpu.CompilerParams(
            collective_id=0, has_side_effects=True, vmem_limit_bytes=55192 * 1024),
        name="floquet",
    )(propagators, perturbation)


def solution(mesh):
    split = Mesh(mesh.devices.reshape(NX, NY, 2, NZ), AXES)
    tm = ("x", "y", "c")
    return jax.shard_map(
        body,
        mesh=split,
        in_specs=(P(tm, None, None), P(tm, "z", None)),
        out_specs=P(tm, None),
        check_vma=False,
    )
```

```python
import jax
import jax.numpy as jnp
from jax import lax
from jax.experimental import pallas as pl
from jax.experimental.pallas import tpu as pltpu
from jax.sharding import Mesh
from jax.sharding import PartitionSpec as P

AXES = ("x", "y", "c", "z")
MESH = pl.DeviceIdType.MESH
F32 = jnp.float32
BF16 = jnp.bfloat16
D = 384
HALF = D // 2
CHUNK = HALF // 2
PART = CHUNK // 2
NX = 4
NY = 4
NZ = 16
FIRST = 1
NW = 2
HB = D // NZ
ROWS = D // 32
UNIT = 16
SUB = NX // NW
PIECE = SUB * UNIT
WIDE = 4 * PIECE
NN = ((1,), (0,))
NT = ((1,), (1,))
TN = ((0,), (0,))


def parts(value):
    high = value.astype(BF16)
    return high, (value - high.astype(F32)).astype(BF16)


def bdot(left, right, dims):
    return lax.dot_general(left, right, (dims, ((), ())), preferred_element_type=F32)


def times(left, right, dims=NN):
    lh, ll = parts(left)
    rh, rl = parts(right)
    if dims is TN:
        return bdot(lh, rh, dims) + (bdot(ll, rh, dims) + bdot(lh, rl, dims))
    n = left.shape[0]
    both = bdot(jnp.concatenate([lh, ll], axis=0), rh, dims)
    return both[:n] + (both[n:] + bdot(lh, rl, dims))


def kernel(a_hbm, h_hbm, o_ref, av, ao, s_buf, r_buf, h_buf, l_buf, z_buf, zo_buf, u_buf, t_buf, v_buf, g_buf, n_buf,
           e_buf, w_buf, f_buf, in_sem, a_sem, ys_sem, yr_sem, yd_sem, ye_sem, xs_sem, xr_sem, xd_sem, xe_sem,
           hs_sem, hr_sem, zz_sem, ts_sem, tr_sem, gs_sem, gr_sem, es_sem, er_sem):
    x, y, c, z = (lax.axis_index(a) for a in AXES)
    worker = (z >= FIRST) & (z < FIRST + NW)
    owner = z == FIRST + lax.div(x, SUB)
    lot = (z - FIRST) * SUB
    here = pl.ds(z * HB, HB)
    a_load = pltpu.make_async_copy(a_hbm.at[0], av, in_sem.at[0])
    h_load = pltpu.make_async_copy(h_hbm.at[0], h_buf.at[here], in_sem.at[1])
    pl.when(worker)(a_load.start)
    h_load.start()
    xr, xl, xo = (lax.rem(x + k, NX) for k in (1, 3, 2))
    yr, yl, yo = (lax.rem(y + k, NY) for k in (1, 3, 2))
    others = [(x, y, c, lax.rem(z + k, NZ)) for k in range(1, NZ)]
    sib = (x, y, 1 - c, z)
    right_y, left_y = (x, yr, c, z), (x, yl, c, z)
    right_x, left_x = (xr, y, c, z), (xl, y, c, z)

    barrier = pltpu.get_barrier_semaphore()

    @pl.when(worker)
    def _():
        for dev in [sib, right_y, left_y, right_x, left_x] + others:
            pl.semaphore_signal(barrier, 1, device_id=dev, device_id_type=MESH)
        pl.semaphore_wait(barrier, 5 + NW - 1)

    @pl.when(jnp.logical_not(worker))
    def _():
        pl.semaphore_wait(barrier, NW)

    def remote(src, dst, send, recv, dev):
        return pltpu.make_async_remote_copy(
            src_ref=src, dst_ref=dst, send_sem=send, recv_sem=recv, device_id=dev, device_id_type=MESH)

    h_out = [remote(h_buf.at[here], h_buf.at[here], hs_sem.at[k], hr_sem.at[0], (x, y, c, FIRST + k))
             for k in range(NW)]

    def send_rows():
        h_load.wait()
        for k, copy in enumerate(h_out):
            pl.when(z != FIRST + k)(copy.start)

    e_out = [remote(e_buf.at[0], e_buf.at[1], es_sem.at[k], er_sem.at[0], dev)
             for k, dev in enumerate(others)]

    def work():
        low, high = pl.ds(0, HALF), pl.ds(HALF, HALF)
        low0, low1 = pl.ds(0, CHUNK), pl.ds(CHUNK, CHUNK)
        half = pl.ds(c * HALF, HALF)

        def a_copies(*where):
            return [remote(av.at[w], ao.at[w], a_sem.at[k], a_sem.at[2 + k], sib) for k, w in enumerate(where)]

        a_down = a_copies(low0, low1)
        top, bottom = pl.ds(0, 256), pl.ds(256, D - 256)
        a_up = a_copies(top, bottom)
        a_load.wait()

        @pl.when(c == 0)
        def _():
            for copy in a_up:
                copy.start()

        @pl.when(c == 1)
        def _():
            for copy in a_down:
                copy.start()
        send_rows()

        def rows(k, core=None):
            return pl.ds((c if core is None else core) * HALF + k * CHUNK, CHUNK)

        def subrows(k, core=None):
            return pl.ds((c if core is None else core) * HALF + k * PART, PART)

        def gather(buf, out_sem, in_sem, share_out, share_in, right, left):
            def copy(place, k, dev, n):
                there = buf.at[place, rows(k) if n < 4 else subrows(k)]
                return remote(there, there, out_sem.at[n], in_sem.at[n], dev)

            def share(place, k, n):
                there = buf.at[place, subrows(k) if 4 <= n < 8 else rows(k)]
                return remote(there, there, share_out.at[n], share_in.at[n], sib)

            def shared(place, k, n):
                there = buf.at[place, subrows(k, 1 - c) if 4 <= n < 8 else rows(k, 1 - c)]
                return remote(there, there, share_out.at[n], share_in.at[n], sib)

            return copy, share, shared

        y_copy, y_share, y_shared = gather(s_buf, ys_sem, yr_sem, yd_sem, ye_sem, right_y, left_y)
        y_out = [
            y_copy(y, 0, right_y, 0), y_copy(y, 1, left_y, 3),
            y_copy(y, 1, right_y, 1), y_copy(y, 0, left_y, 2),
        ]
        y_sh = {}

        def share_s(place, k, n):
            copy = y_share(place, k, n)
            copy.start()
            y_sh[n] = (copy, y_shared(place, k, n))

        @pl.when(c == 0)
        def _():
            a_down[0].wait_recv()
            s_buf[y, low0] = times(ao[low0], av[...])
            y_out[0].start()
            a_down[1].wait_recv()
            s_buf[y, low1] = times(ao[low1], av[...])

        @pl.when(c == 1)
        def _():
            a_up[0].wait_recv()
            value = times(av[high, top], ao[top])
            a_up[1].wait_recv()
            s_buf[y, high] = value + times(av[high, bottom], ao[bottom])
            y_out[0].start()

        for copy in y_out[1:]:
            copy.start()
        share_s(y, 0, 8)
        share_s(y, 1, 9)

        def relay(k, source, dev, n):
            for m in range(2):
                copy = y_copy(source, 2 * k + m, dev, n + m)
                copy.start()
                y_out.append(copy)

        y_copy(yl, 0, left_y, 0).wait_recv()
        relay(0, yl, right_y, 4)
        y_copy(yr, 1, right_y, 3).wait_recv()
        relay(1, yr, left_y, 6)
        share_s(yl, 0, 0)
        share_s(yr, 1, 3)
        y_copy(yl, 1, left_y, 1).wait_recv()
        share_s(yl, 1, 1)
        y_copy(yr, 0, left_y, 2).wait_recv()
        share_s(yr, 0, 2)
        for k, n in ((0, 4), (2, 6), (1, 5), (3, 7)):
            y_copy(yo, k, left_y, n).wait_recv()
            share_s(yo, k, n)

        for n in (8, 9, 0, 3, 1, 2):
            y_sh[n][1].wait_recv()

        ahead = x < NX - 1

        @pl.when(ahead & (y == 0))
        def _():
            z_buf[...] = times(s_buf[1], s_buf[0])

        @pl.when(ahead & (y == 1))
        def _():
            z_buf[...] = times(s_buf[2], times(s_buf[1], s_buf[0]))

        @pl.when(ahead & (y >= 2))
        def _():
            n_buf[...] = times(s_buf[3, half], s_buf[2])

        @pl.when(ahead & (y == 2))
        def _():
            n_buf[...] = times(n_buf[...], s_buf[1])

        def opposite_shared():
            for n in (4, 6, 5, 7):
                y_sh[n][1].wait_recv()

        pl.when(y != 1)(opposite_shared)

        @pl.when(ahead & (y == 0))
        def _():
            r_buf[x, half] = times(times(s_buf[3, half], s_buf[2]), z_buf[...])

        @pl.when(ahead & (y == 1))
        def _():
            r_buf[x, half] = times(s_buf[3, half], z_buf[...])

        @pl.when(ahead & (y == 2))
        def _():
            r_buf[x, half] = times(n_buf[...], s_buf[0])

        @pl.when(ahead & (y == 3))
        def _():
            r_buf[x, half] = times(times(n_buf[...], s_buf[1]), s_buf[0])

        x_copy, x_share, x_shared = gather(r_buf, xs_sem, xr_sem, xd_sem, xe_sem, right_x, left_x)

        to_right = x < 3
        first = x == 0
        last = x == 3
        x_out = []

        def when_start(cond, copy):
            @pl.when(cond)
            def _():
                copy.start()
            x_out.append((cond, copy))

        def when_recv(cond, copy):
            @pl.when(cond)
            def _():
                copy.wait_recv()

        when_start(to_right, x_copy(x, 0, right_x, 0))
        when_start(x < 2, x_copy(x, 1, left_x, 3))
        when_start(to_right, x_copy(x, 1, right_x, 1))
        when_start(first, x_copy(x, 0, left_x, 2))
        pl.when(y == 1)(opposite_shared)

        @pl.when(y == 1)
        def _():
            l_buf[...] = s_buf[0]

        @pl.when(y >= 2)
        def _():
            l_buf[...] = times(s_buf[1], s_buf[0])

        @pl.when((c == 1) & (y == 0))
        def _():
            l_buf[...] = ao[...]

        @pl.when(y == 3)
        def _():
            l_buf[...] = times(s_buf[2], l_buf[...])

        @pl.when((c == 1) & (y > 0))
        def _():
            l_buf[...] = times(ao[...], l_buf[...])

        x_sh = {}

        def share_r(cond, place, k, n):
            copy = x_share(place, k, n)
            when_start(cond, copy)
            x_sh[n] = (cond, x_shared(place, k, n))

        from_left = x > 0
        opposite = x > 1
        when_recv(from_left, x_copy(xl, 0, left_x, 0))
        for m in range(2):
            when_start((x == 1) | (x == 2), x_copy(xl, m, right_x, 4 + m))
        when_recv(first | last, x_copy(xr, 1, right_x, 3))
        for m in range(2):
            when_start(first | last, x_copy(xr, 2 + m, left_x, 6 + m))
        share_r(from_left, xl, 0, 0)
        share_r(last, xr, 1, 3)

        rest = h_buf.at[pl.ds(0, (NZ - 1) * HB)]
        remote(rest, rest, hs_sem.at[0], hr_sem.at[0], sib).wait_recv()
        inner = (y > 0) | (c > 0)

        @pl.when(jnp.logical_not(inner))
        def _():
            z_buf[...] = h_buf[...]

        @pl.when(inner)
        def _():
            z_buf[...] = times(l_buf[...], times(h_buf[...], l_buf[...]), TN)

        z_copy = remote(z_buf, zo_buf, zz_sem.at[0], zz_sem.at[1], sib)
        z_copy.start()

        when_recv(from_left, x_copy(xl, 1, left_x, 1))
        share_r(from_left, xl, 1, 1)
        when_recv(last, x_copy(xr, 0, left_x, 2))
        share_r(last, xr, 0, 2)

        place = lax.broadcasted_iota(jnp.int32, (WIDE, D), 0)
        column = lax.broadcasted_iota(jnp.int32, (WIDE, D), 1)
        within = lax.rem(place, UNIT)
        block = lot + lax.rem(lax.div(place, UNIT), SUB)
        wanted = block * (8 * ROWS) + (lax.div(place, PIECE) * 2 + c) * ROWS + within
        u_buf[...] = jnp.where((within < ROWS) & (column == wanted), 1.0, 0.0).astype(F32)
        for n in (0, 3, 1, 2):
            when_recv(*x_sh[n])

        @pl.when((x == 1) | last)
        def _():
            u_buf[...] = times(u_buf[...], r_buf[0], NT)

        for k, n in ((0, 4), (2, 6), (1, 5), (3, 7)):
            when_recv(opposite, x_copy(xo, k, left_x, n))
            share_r(opposite, xo, k, n)

        z_copy.wait_recv()
        z_copy.wait_send()
        z_buf[...] = z_buf[...] + zo_buf[...]

        @pl.when(x == 2)
        def _():
            z_buf[...] = times(r_buf[1], z_buf[...], TN)

        @pl.when(x == 3)
        def _():
            z_buf[...] = times(r_buf[2], z_buf[...], TN)
        for n in (4, 6, 5, 7):
            when_recv(*x_sh[n])

        @pl.when(x == 2)
        def _():
            u_buf[...] = times(u_buf[...], r_buf[0], NT)

        @pl.when(x == 3)
        def _():
            u_buf[...] = times(u_buf[...], r_buf[1], NT)
        u_buf[...] = times(u_buf[...], z_buf[...])

        t_out = []
        for q in range(4):
            for k in range(SUB):
                w_buf[q, k] = u_buf[pl.ds(q * PIECE + k * UNIT, ROWS)]
        for q in range(4):
            mine = y == q
            copy = remote(w_buf.at[q], t_buf.at[y], ts_sem.at[q], tr_sem.at[y], (x, q, c, z))

            @pl.when(mine)
            def _(q=q):
                t_buf[y] = w_buf[q]

            @pl.when(jnp.logical_not(mine))
            def _(copy=copy):
                copy.start()
            t_out.append((jnp.logical_not(mine), copy))

        v_buf[...] = jnp.zeros((PIECE, D), F32)

        @pl.when(x >= 2)
        def _():
            l_buf[...] = times(r_buf[1], r_buf[0])

        @pl.when(x == 3)
        def _():
            l_buf[...] = times(r_buf[2], l_buf[...])
        for k in range(NY):
            @pl.when(y != k)
            def _(k=k):
                remote(t_buf.at[k], t_buf.at[k], ts_sem.at[0], tr_sem.at[k], sib).wait_recv()
        for k in range(SUB):
            v_buf[pl.ds(k * UNIT, ROWS)] = (t_buf[0, k] + t_buf[1, k]) + (t_buf[2, k] + t_buf[3, k])
        value = v_buf[...]

        def place_pieces(value):
            for k in range(SUB):
                f_buf[k] = value[k * UNIT:k * UNIT + ROWS]

        @pl.when(x == 0)
        def _():
            place_pieces(value)

        @pl.when(x == 1)
        def _():
            place_pieces(times(value, r_buf[0]))

        @pl.when(x >= 2)
        def _():
            place_pieces(times(value, l_buf[...]))

        for k in range(SUB):
            there = lot + k
            copy = remote(f_buf.at[k], g_buf.at[x], gs_sem.at[k], gr_sem.at[x], (there, y, c, z))
            pl.when(x != there)(copy.start)
            t_out.append((x != there, copy))

        @pl.when(owner)
        def _():
            total = f_buf[x - lot]
            for k in (1, 3, 2):
                k = lax.rem(x + k, NX)
                remote(g_buf.at[k], g_buf.at[k], gs_sem.at[0], gr_sem.at[k], sib).wait_recv()
            for k in (1, 3, 2):
                total = total + g_buf[lax.rem(x + k, NX)]
            e_buf[0] = total
            for k in (14, 13, 0, 1, 2, 3, 4, 12, 5, 11, 10, 6, 7, 8, 9):
                e_out[k].start()
            o_ref[...] = total

        @pl.when(c == 0)
        def _():
            for copy in a_up:
                copy.wait_send()

        @pl.when(c == 1)
        def _():
            for copy in a_down:
                copy.wait_send()
        for copy in y_out:
            copy.wait_send()
        for copy, _ in y_sh.values():
            copy.wait_send()
        for cond, copy in x_out + t_out:
            pl.when(cond)(copy.wait_send)

    @pl.when(worker)
    def _():
        work()

    @pl.when(jnp.logical_not(worker))
    def _():
        send_rows()

    @pl.when(owner)
    def _():
        for copy in e_out:
            copy.wait_send()

    @pl.when(jnp.logical_not(owner))
    def _():
        e_out[0].wait_recv()
        o_ref[...] = e_buf[1]

    for k, copy in enumerate(h_out):
        pl.when(z != FIRST + k)(copy.wait_send)


def body(propagators, perturbation):
    full = pltpu.VMEM((D, D), F32)
    dma = pltpu.SemaphoreType.DMA
    return pl.pallas_call(
        kernel,
        out_shape=jax.ShapeDtypeStruct((ROWS, D), F32),
        in_specs=[pl.BlockSpec(memory_space=pltpu.HBM)] * 2,
        out_specs=pl.BlockSpec(memory_space=pltpu.VMEM),
        scratch_shapes=[
            full, full,
            pltpu.VMEM((NY, D, D), F32),
            pltpu.VMEM((NX, D, D), F32),
            full, full, full, full,
            pltpu.VMEM((WIDE, D), F32),
            pltpu.VMEM((NY, SUB, ROWS, D), F32),
            pltpu.VMEM((PIECE, D), F32),
            pltpu.VMEM((NX, ROWS, D), F32),
            pltpu.VMEM((HALF, D), F32),
            pltpu.VMEM((2, ROWS, D), F32),
            pltpu.VMEM((4, SUB, ROWS, D), F32),
            pltpu.VMEM((SUB, ROWS, D), F32),
            dma((2,)), dma((4,)),
            dma((8,)), dma((8,)), dma((10,)), dma((10,)),
            dma((8,)), dma((8,)), dma((8,)), dma((8,)),
            dma((NW,)), dma((1,)), dma((2,)),
            dma((4,)), dma((4,)),
            dma((SUB,)), dma((4,)),
            dma((NZ - 1,)), dma((1,)),
        ],
        compiler_params=pltpu.CompilerParams(
            collective_id=0, has_side_effects=True, vmem_limit_bytes=55192 * 1024),
        name="floquet",
    )(propagators, perturbation)


def solution(mesh):
    split = Mesh(mesh.devices.reshape(NX, NY, 2, NZ), AXES)
    tm = ("x", "y", "c")
    return jax.shard_map(
        body,
        mesh=split,
        in_specs=(P(tm, None, None), P(tm, "z", None)),
        out_specs=P(tm, None),
        check_vma=False,
    )
```

```python
import jax
import jax.numpy as jnp
from jax import lax
from jax.experimental import pallas as pl
from jax.experimental.pallas import tpu as pltpu
from jax.sharding import Mesh
from jax.sharding import PartitionSpec as P

AXES = ("x", "y", "c", "z")
MESH = pl.DeviceIdType.MESH
F32 = jnp.float32
BF16 = jnp.bfloat16
D = 384
HALF = D // 2
CHUNK = HALF // 2
PART = CHUNK // 2
NX = 4
NY = 4
NZ = 16
FIRST = 1
NW = 2
HB = D // NZ
ROWS = D // 32
UNIT = 16
SUB = NX // NW
PIECE = SUB * UNIT
WIDE = 4 * PIECE
NN = ((1,), (0,))
NT = ((1,), (1,))
TN = ((0,), (0,))


def parts(value):
    high = value.astype(BF16)
    return high, (value - high.astype(F32)).astype(BF16)


def bdot(left, right, dims):
    return lax.dot_general(left, right, (dims, ((), ())), preferred_element_type=F32)


def times(left, right, dims=NN):
    lh, ll = parts(left)
    rh, rl = parts(right)
    if dims is TN:
        return bdot(lh, rh, dims) + (bdot(ll, rh, dims) + bdot(lh, rl, dims))
    n = left.shape[0]
    both = bdot(jnp.concatenate([lh, ll], axis=0), rh, dims)
    return both[:n] + (both[n:] + bdot(lh, rl, dims))


def kernel(a_hbm, h_hbm, o_ref, av, ao, s_buf, r_buf, h_buf, l_buf, z_buf, zo_buf, u_buf, t_buf, v_buf, g_buf, n_buf,
           e_buf, w_buf, f_buf, in_sem, a_sem, ys_sem, yr_sem, yd_sem, ye_sem, xs_sem, xr_sem, xd_sem, xe_sem,
           hs_sem, hr_sem, zz_sem, ts_sem, tr_sem, gs_sem, gr_sem, es_sem, er_sem):
    x, y, c, z = (lax.axis_index(a) for a in AXES)
    worker = (z >= FIRST) & (z < FIRST + NW)
    owner = z == FIRST + lax.div(x, SUB)
    lot = (z - FIRST) * SUB
    here = pl.ds(z * HB, HB)
    a_load = pltpu.make_async_copy(a_hbm.at[0], av, in_sem.at[0])
    h_load = pltpu.make_async_copy(h_hbm.at[0], h_buf.at[here], in_sem.at[1])
    pl.when(worker)(a_load.start)
    h_load.start()
    xr, xl, xo = (lax.rem(x + k, NX) for k in (1, 3, 2))
    yr, yl, yo = (lax.rem(y + k, NY) for k in (1, 3, 2))
    others = [(x, y, c, lax.rem(z + k, NZ)) for k in range(1, NZ)]
    sib = (x, y, 1 - c, z)
    right_y, left_y = (x, yr, c, z), (x, yl, c, z)
    right_x, left_x = (xr, y, c, z), (xl, y, c, z)

    barrier = pltpu.get_barrier_semaphore()

    @pl.when(worker)
    def _():
        for dev in [sib, right_y, left_y, right_x, left_x] + others:
            pl.semaphore_signal(barrier, 1, device_id=dev, device_id_type=MESH)
        pl.semaphore_wait(barrier, 5 + NW - 1)

    @pl.when(jnp.logical_not(worker))
    def _():
        pl.semaphore_wait(barrier, NW)

    def remote(src, dst, send, recv, dev):
        return pltpu.make_async_remote_copy(
            src_ref=src, dst_ref=dst, send_sem=send, recv_sem=recv, device_id=dev, device_id_type=MESH)

    h_out = [remote(h_buf.at[here], h_buf.at[here], hs_sem.at[k], hr_sem.at[0], (x, y, c, FIRST + k))
             for k in range(NW)]

    def send_rows():
        h_load.wait()
        for k, copy in enumerate(h_out):
            pl.when(z != FIRST + k)(copy.start)

    e_out = [remote(e_buf.at[0], e_buf.at[1], es_sem.at[k], er_sem.at[0], dev)
             for k, dev in enumerate(others)]

    def work():
        low, high = pl.ds(0, HALF), pl.ds(HALF, HALF)
        low0, low1 = pl.ds(0, CHUNK), pl.ds(CHUNK, CHUNK)
        half = pl.ds(c * HALF, HALF)

        def a_copies(*where):
            return [remote(av.at[w], ao.at[w], a_sem.at[k], a_sem.at[2 + k], sib) for k, w in enumerate(where)]

        a_down = a_copies(low0, low1)
        top, bottom = pl.ds(0, 256), pl.ds(256, D - 256)
        a_up = a_copies(top, bottom)
        a_load.wait()

        @pl.when(c == 0)
        def _():
            for copy in a_up:
                copy.start()

        @pl.when(c == 1)
        def _():
            for copy in a_down:
                copy.start()
        send_rows()

        def rows(k, core=None):
            return pl.ds((c if core is None else core) * HALF + k * CHUNK, CHUNK)

        def subrows(k, core=None):
            return pl.ds((c if core is None else core) * HALF + k * PART, PART)

        def gather(buf, out_sem, in_sem, share_out, share_in, right, left):
            def copy(place, k, dev, n):
                there = buf.at[place, rows(k) if n < 4 else subrows(k)]
                return remote(there, there, out_sem.at[n], in_sem.at[n], dev)

            def share(place, k, n):
                there = buf.at[place, subrows(k) if 4 <= n < 8 else rows(k)]
                return remote(there, there, share_out.at[n], share_in.at[n], sib)

            def shared(place, k, n):
                there = buf.at[place, subrows(k, 1 - c) if 4 <= n < 8 else rows(k, 1 - c)]
                return remote(there, there, share_out.at[n], share_in.at[n], sib)

            return copy, share, shared

        y_copy, y_share, y_shared = gather(s_buf, ys_sem, yr_sem, yd_sem, ye_sem, right_y, left_y)
        y_out = [
            y_copy(y, 0, right_y, 0), y_copy(y, 1, left_y, 3),
            y_copy(y, 1, right_y, 1), y_copy(y, 0, left_y, 2),
        ]
        y_sh = {}

        def share_s(place, k, n):
            copy = y_share(place, k, n)
            copy.start()
            y_sh[n] = (copy, y_shared(place, k, n))

        @pl.when(c == 0)
        def _():
            a_down[0].wait_recv()
            s_buf[y, low0] = times(ao[low0], av[...])
            y_out[0].start()
            a_down[1].wait_recv()
            s_buf[y, low1] = times(ao[low1], av[...])

        @pl.when(c == 1)
        def _():
            a_up[0].wait_recv()
            value = times(av[high, top], ao[top])
            a_up[1].wait_recv()
            s_buf[y, high] = value + times(av[high, bottom], ao[bottom])
            y_out[0].start()

        for copy in y_out[1:]:
            copy.start()
        share_s(y, 0, 8)
        share_s(y, 1, 9)

        def relay(k, source, dev, n):
            for m in range(2):
                copy = y_copy(source, 2 * k + m, dev, n + m)
                copy.start()
                y_out.append(copy)

        y_copy(yl, 0, left_y, 0).wait_recv()
        relay(0, yl, right_y, 4)
        y_copy(yr, 1, right_y, 3).wait_recv()
        relay(1, yr, left_y, 6)
        share_s(yl, 0, 0)
        share_s(yr, 1, 3)
        y_copy(yl, 1, left_y, 1).wait_recv()
        share_s(yl, 1, 1)
        y_copy(yr, 0, left_y, 2).wait_recv()
        share_s(yr, 0, 2)
        for k, n in ((0, 4), (2, 6), (1, 5), (3, 7)):
            y_copy(yo, k, left_y, n).wait_recv()
            share_s(yo, k, n)

        for n in (8, 9, 0, 3, 1, 2):
            y_sh[n][1].wait_recv()

        ahead = x < NX - 1

        @pl.when(ahead & (y == 0))
        def _():
            z_buf[...] = times(s_buf[1], s_buf[0])

        @pl.when(ahead & (y == 1))
        def _():
            z_buf[...] = times(s_buf[2], times(s_buf[1], s_buf[0]))

        @pl.when(ahead & (y >= 2))
        def _():
            n_buf[...] = times(s_buf[3, half], s_buf[2])

        @pl.when(ahead & (y == 2))
        def _():
            n_buf[...] = times(n_buf[...], s_buf[1])

        def opposite_shared():
            for n in (4, 6, 5, 7):
                y_sh[n][1].wait_recv()

        pl.when(y != 1)(opposite_shared)

        @pl.when(ahead & (y == 0))
        def _():
            r_buf[x, half] = times(times(s_buf[3, half], s_buf[2]), z_buf[...])

        @pl.when(ahead & (y == 1))
        def _():
            r_buf[x, half] = times(s_buf[3, half], z_buf[...])

        @pl.when(ahead & (y == 2))
        def _():
            r_buf[x, half] = times(n_buf[...], s_buf[0])

        @pl.when(ahead & (y == 3))
        def _():
            r_buf[x, half] = times(times(n_buf[...], s_buf[1]), s_buf[0])

        x_copy, x_share, x_shared = gather(r_buf, xs_sem, xr_sem, xd_sem, xe_sem, right_x, left_x)

        to_right = x < 3
        first = x == 0
        last = x == 3
        x_out = []

        def when_start(cond, copy):
            @pl.when(cond)
            def _():
                copy.start()
            x_out.append((cond, copy))

        def when_recv(cond, copy):
            @pl.when(cond)
            def _():
                copy.wait_recv()

        when_start(to_right, x_copy(x, 0, right_x, 0))
        when_start(x < 2, x_copy(x, 1, left_x, 3))
        when_start(to_right, x_copy(x, 1, right_x, 1))
        when_start(first, x_copy(x, 0, left_x, 2))
        pl.when(y == 1)(opposite_shared)

        @pl.when(y == 1)
        def _():
            l_buf[...] = s_buf[0]

        @pl.when(y >= 2)
        def _():
            l_buf[...] = times(s_buf[1], s_buf[0])

        @pl.when((c == 1) & (y == 0))
        def _():
            l_buf[...] = ao[...]

        @pl.when(y == 3)
        def _():
            l_buf[...] = times(s_buf[2], l_buf[...])

        @pl.when((c == 1) & (y > 0))
        def _():
            l_buf[...] = times(ao[...], l_buf[...])

        x_sh = {}

        def share_r(cond, place, k, n):
            copy = x_share(place, k, n)
            when_start(cond, copy)
            x_sh[n] = (cond, x_shared(place, k, n))

        from_left = x > 0
        opposite = x > 1
        when_recv(from_left, x_copy(xl, 0, left_x, 0))
        for m in range(2):
            when_start((x == 1) | (x == 2), x_copy(xl, m, right_x, 4 + m))
        when_recv(first | last, x_copy(xr, 1, right_x, 3))
        for m in range(2):
            when_start(first | last, x_copy(xr, 2 + m, left_x, 6 + m))
        share_r(from_left, xl, 0, 0)
        share_r(last, xr, 1, 3)

        rest = h_buf.at[pl.ds(0, (NZ - 1) * HB)]
        remote(rest, rest, hs_sem.at[0], hr_sem.at[0], sib).wait_recv()
        inner = (y > 0) | (c > 0)

        @pl.when(jnp.logical_not(inner))
        def _():
            z_buf[...] = h_buf[...]

        @pl.when(inner)
        def _():
            z_buf[...] = times(l_buf[...], times(h_buf[...], l_buf[...]), TN)

        z_copy = remote(z_buf, zo_buf, zz_sem.at[0], zz_sem.at[1], sib)
        z_copy.start()

        when_recv(from_left, x_copy(xl, 1, left_x, 1))
        share_r(from_left, xl, 1, 1)
        when_recv(last, x_copy(xr, 0, left_x, 2))
        share_r(last, xr, 0, 2)

        place = lax.broadcasted_iota(jnp.int32, (WIDE, D), 0)
        column = lax.broadcasted_iota(jnp.int32, (WIDE, D), 1)
        within = lax.rem(place, UNIT)
        block = lot + lax.rem(lax.div(place, UNIT), SUB)
        wanted = block * (8 * ROWS) + (lax.div(place, PIECE) * 2 + c) * ROWS + within
        u_buf[...] = jnp.where((within < ROWS) & (column == wanted), 1.0, 0.0).astype(F32)
        for n in (0, 3, 1, 2):
            when_recv(*x_sh[n])

        @pl.when((x == 1) | last)
        def _():
            u_buf[...] = times(u_buf[...], r_buf[0], NT)

        for k, n in ((0, 4), (2, 6), (1, 5), (3, 7)):
            when_recv(opposite, x_copy(xo, k, left_x, n))
            share_r(opposite, xo, k, n)

        z_copy.wait_recv()
        z_copy.wait_send()
        z_buf[...] = z_buf[...] + zo_buf[...]

        @pl.when(x == 2)
        def _():
            z_buf[...] = times(r_buf[1], z_buf[...], TN)

        @pl.when(x == 3)
        def _():
            z_buf[...] = times(r_buf[2], z_buf[...], TN)
        for n in (4, 6, 5, 7):
            when_recv(*x_sh[n])

        @pl.when(x == 2)
        def _():
            u_buf[...] = times(u_buf[...], r_buf[0], NT)

        @pl.when(x == 3)
        def _():
            u_buf[...] = times(u_buf[...], r_buf[1], NT)

        t_out = []
        for q in range(4):
            if q % 2 == 0:
                value = times(u_buf[pl.ds(q * PIECE, 2 * PIECE)], z_buf[...])
                for k in range(2 * SUB):
                    w_buf[q + k // SUB, k % SUB] = value[k * UNIT:k * UNIT + ROWS]
            mine = y == q
            copy = remote(w_buf.at[q], t_buf.at[y], ts_sem.at[q], tr_sem.at[y], (x, q, c, z))

            @pl.when(mine)
            def _(q=q):
                t_buf[y] = w_buf[q]

            @pl.when(jnp.logical_not(mine))
            def _(copy=copy):
                copy.start()
            t_out.append((jnp.logical_not(mine), copy))

        v_buf[...] = jnp.zeros((PIECE, D), F32)

        @pl.when(x >= 2)
        def _():
            l_buf[...] = times(r_buf[1], r_buf[0])

        @pl.when(x == 3)
        def _():
            l_buf[...] = times(r_buf[2], l_buf[...])
        for k in range(NY):
            @pl.when(y != k)
            def _(k=k):
                remote(t_buf.at[k], t_buf.at[k], ts_sem.at[0], tr_sem.at[k], sib).wait_recv()
        for k in range(SUB):
            v_buf[pl.ds(k * UNIT, ROWS)] = (t_buf[0, k] + t_buf[1, k]) + (t_buf[2, k] + t_buf[3, k])
        value = v_buf[...]

        def place_pieces(value):
            for k in range(SUB):
                f_buf[k] = value[k * UNIT:k * UNIT + ROWS]

        @pl.when(x == 0)
        def _():
            place_pieces(value)

        @pl.when(x == 1)
        def _():
            place_pieces(times(value, r_buf[0]))

        @pl.when(x >= 2)
        def _():
            place_pieces(times(value, l_buf[...]))

        for k in range(SUB):
            there = lot + k
            copy = remote(f_buf.at[k], g_buf.at[x], gs_sem.at[k], gr_sem.at[x], (there, y, c, z))
            pl.when(x != there)(copy.start)
            t_out.append((x != there, copy))

        @pl.when(owner)
        def _():
            total = f_buf[x - lot]
            for k in (1, 3, 2):
                k = lax.rem(x + k, NX)
                remote(g_buf.at[k], g_buf.at[k], gs_sem.at[0], gr_sem.at[k], sib).wait_recv()
            for k in (1, 3, 2):
                total = total + g_buf[lax.rem(x + k, NX)]
            e_buf[0] = total
            for k in (14, 13, 0, 1, 2, 3, 4, 12, 5, 11, 10, 6, 7, 8, 9):
                e_out[k].start()
            o_ref[...] = total

        @pl.when(c == 0)
        def _():
            for copy in a_up:
                copy.wait_send()

        @pl.when(c == 1)
        def _():
            for copy in a_down:
                copy.wait_send()
        for copy in y_out:
            copy.wait_send()
        for copy, _ in y_sh.values():
            copy.wait_send()
        for cond, copy in x_out + t_out:
            pl.when(cond)(copy.wait_send)

    @pl.when(worker)
    def _():
        work()

    @pl.when(jnp.logical_not(worker))
    def _():
        send_rows()

    @pl.when(owner)
    def _():
        for copy in e_out:
            copy.wait_send()

    @pl.when(jnp.logical_not(owner))
    def _():
        e_out[0].wait_recv()
        o_ref[...] = e_buf[1]

    for k, copy in enumerate(h_out):
        pl.when(z != FIRST + k)(copy.wait_send)


def body(propagators, perturbation):
    full = pltpu.VMEM((D, D), F32)
    dma = pltpu.SemaphoreType.DMA
    return pl.pallas_call(
        kernel,
        out_shape=jax.ShapeDtypeStruct((ROWS, D), F32),
        in_specs=[pl.BlockSpec(memory_space=pltpu.HBM)] * 2,
        out_specs=pl.BlockSpec(memory_space=pltpu.VMEM),
        scratch_shapes=[
            full, full,
            pltpu.VMEM((NY, D, D), F32),
            pltpu.VMEM((NX, D, D), F32),
            full, full, full, full,
            pltpu.VMEM((WIDE, D), F32),
            pltpu.VMEM((NY, SUB, ROWS, D), F32),
            pltpu.VMEM((PIECE, D), F32),
            pltpu.VMEM((NX, ROWS, D), F32),
            pltpu.VMEM((HALF, D), F32),
            pltpu.VMEM((2, ROWS, D), F32),
            pltpu.VMEM((4, SUB, ROWS, D), F32),
            pltpu.VMEM((SUB, ROWS, D), F32),
            dma((2,)), dma((4,)),
            dma((8,)), dma((8,)), dma((10,)), dma((10,)),
            dma((8,)), dma((8,)), dma((8,)), dma((8,)),
            dma((NW,)), dma((1,)), dma((2,)),
            dma((4,)), dma((4,)),
            dma((SUB,)), dma((4,)),
            dma((NZ - 1,)), dma((1,)),
        ],
        compiler_params=pltpu.CompilerParams(
            collective_id=0, has_side_effects=True, vmem_limit_bytes=55192 * 1024),
        name="floquet",
    )(propagators, perturbation)


def solution(mesh):
    split = Mesh(mesh.devices.reshape(NX, NY, 2, NZ), AXES)
    tm = ("x", "y", "c")
    return jax.shard_map(
        body,
        mesh=split,
        in_specs=(P(tm, None, None), P(tm, "z", None)),
        out_specs=P(tm, None),
        check_vma=False,
    )
```
